256 devices in a mesh: wide: 32 (over y, z), narrow: 8 (over x, core).
Axes of the slice: x: 4, y: 4, z: 8, core: 2. Of those that a mesh axis runs over, the one named last changes fastest.
Arguments:
- obs_blocks: bfloat16 [32, 128, 512, 512], P('wide', None, 'narrow'), may hold values from -6 to 6
- obs_row: int32 [32, 128], P('wide'), may hold values from 0 to 7, never falling along the last dimension, each value on 1 to 32 neighbouring positions
- obs_col: int32 [32, 128], P('wide'), may hold values from 0 to 255
- factors: bfloat16 [256, 512, 256], P('wide', 'narrow'), may hold values from -0.25 to 0.25
Outputs:
- agent_factors: float32 [256, 512, 256], P(('wide', 'narrow'))
The draws below stay inside these ranges and needn't reach their ends.
Inputs may be any that keep to these rules, and one draw needn't show every extreme that they name: `obs_row`: within each group the rows never fall along the slots; every row 0 to 7 has 1 to 32 slots, and some row exactly 32. `obs_col`: any opponent block, repeats allowed.
All inputs are finite; a program needn't handle non-finite values.
Results may differ from the reference program's by a relative error of at most 0.0003.
Values may be sent and summed in bfloat16 or wider, within the bound.
A program may use at most 128 MiB of HBM per device.

```python
import math
import jax
import jax.numpy as jnp
import numpy as np
from jax import lax

B = 512
R = 256
RW = 8
KD = 128
MOST = 32
NO = 256
NA = 256
N_WIDE = 32
N_NARROW = 8


def touch_ends(drawn, rng, least, largest):
    index_at = [jax.random.randint(jax.random.fold_in(rng, axis), (), 0, length) for axis, length in enumerate(drawn.shape)]
    widest = drawn.shape.index(max(drawn.shape))
    neighbour = index_at[:widest] + [(index_at[widest] + 1) % drawn.shape[widest]] + index_at[widest + 1:]
    return drawn.at[tuple(index_at)].set(least).at[tuple(neighbour)].set(largest)


def block_scale(key, dims, pieces, low, largest):
    gain = 1.0
    for dim, shards_of in pieces:
        draws = jax.random.uniform(jax.random.fold_in(jax.random.fold_in(key, 6), dim), (shards_of,), jnp.float32, low / len(pieces), largest / len(pieces))
        gain = gain * jnp.repeat(jnp.exp(draws), dims[dim] // shards_of).reshape((-1,) + (1,) * (len(dims) - 1 - dim))
    return gain


def length_profile(number_of, total, limit, skew):
    weights = [(1 << 20) // math.isqrt(standing ** skew) + 1 for standing in range(2, number_of + 1)]
    surplus, given = total - limit - (number_of - 1), [1] * (number_of - 1)
    while surplus > 0:
        movable = [i for i in range(number_of - 1) if given[i] < limit]
        pool, budget = sum([weights[i] for i in movable]), surplus
        for i in movable:
            more = min(limit - given[i], max(1, budget * weights[i] // pool), surplus)
            given[i] = given[i] + more
            surplus = surplus - more
    return np.array([limit] + given)


def ragged(own_key, count, total, bound, lean):
    if count == 2:
        one = jax.random.randint(own_key, (), max(1, total - bound), min(bound, total - 1) + 1)
        return jnp.stack([one, total - one])
    tallies = jnp.asarray(length_profile(count, total, bound, lean), jnp.int32)
    twos = (count - 1) // 2
    giver, taker = tallies[1:1 + 2 * twos:2], tallies[2:2 + 2 * twos:2]
    room = jnp.minimum(giver - 1, bound - taker)
    passed = jax.random.randint(jax.random.fold_in(own_key, 1), (twos,), 0, 1 << 20) % (room + 1)
    tallies = tallies.at[1:1 + 2 * twos:2].set(giver - passed).at[2:2 + 2 * twos:2].set(taker + passed)
    return tallies[jax.random.permutation(jax.random.fold_in(own_key, 2), count)]


def centred(stream_key, extent, spread, bound, split=(), held_as=jnp.bfloat16):
    gain = block_scale(stream_key, extent, split, -0.22, 0.18) if split else 1.0
    drawn = jax.random.normal(stream_key, extent, jnp.float32) * spread * gain
    return jnp.minimum(jnp.maximum(drawn, -bound), bound).astype(held_as)


def setup_inputs(seed: int = 0) -> dict:
    seeds = jax.random.split(jax.random.key(seed), 5)
    return {
        "obs_blocks": centred(seeds[0], (N_WIDE, KD, B, B), 1.0, 6.0, ((0, 32), (2, 8))),
        "obs_row": jax.vmap(lambda own: jnp.searchsorted(jnp.cumsum(ragged(own, RW, KD, MOST, 2)), jnp.arange(KD), side="right"))(jax.random.split(seeds[1], N_WIDE)).reshape((N_WIDE, KD)).astype(jnp.int32),
        "obs_col": touch_ends(jax.random.randint(seeds[2], (N_WIDE, KD), 0, NO), jax.random.fold_in(seeds[2], 1), 0, NO - 1).astype(jnp.int32),
        "factors": centred(seeds[3], (NO, B, R), B ** -0.5, 0.25, ((0, 32), (1, 8))),
    }


LAMBDA_REG = 1.0

def solve_rows(rhs, gram):
    chol = jnp.linalg.cholesky(gram)
    forward = lax.linalg.triangular_solve(chol, rhs, left_side=False, lower=True, transpose_a=True)
    return lax.linalg.triangular_solve(chol, forward, left_side=False, lower=True, transpose_a=False)

def reference(obs_blocks, obs_row, obs_col, factors):
    part = B // N_NARROW
    wide_f = factors.astype(jnp.float32)
    block_gram = jnp.einsum('obr,obs->ors', wide_f, wide_f, precision=lax.Precision.HIGHEST)
    row_hot = (obs_row[:, :, None] == jnp.arange(RW, dtype=jnp.int32)[None, None, :]).astype(jnp.float32)
    col_hot = (obs_col[:, :, None] == jnp.arange(NO, dtype=jnp.int32)[None, None, :]).astype(jnp.float32)
    counts = jnp.einsum('wki,wko->wio', row_hot, col_hot, precision=lax.Precision.HIGHEST)
    gram = jnp.einsum('wio,ors->wirs', counts, block_gram, precision=lax.Precision.HIGHEST)
    gram = gram + LAMBDA_REG * jnp.eye(R, dtype=jnp.float32)[None, None]

    def one_group(items):
        blocks, rows, cols = items
        selected = factors[cols]

        def one_part(index):
            start = (index * part).astype(jnp.int32)
            piece = lax.dynamic_slice_in_dim(blocks, start, part, 1).astype(jnp.float32)
            chosen = lax.dynamic_slice_in_dim(selected, start, part, 1).astype(jnp.float32)
            product = jnp.einsum('kba,kbr->kar', piece, chosen, precision=lax.Precision.HIGHEST)
            return jax.ops.segment_sum(product, rows, num_segments=RW)
        partials = lax.map(one_part, jnp.arange(N_NARROW, dtype=jnp.int32))
        return jnp.sum(partials, axis=0)
    rhs = lax.map(one_group, (obs_blocks, obs_row, obs_col))
    solved = solve_rows(rhs.reshape(NA, B, R), gram.reshape(NA, R, R))
    return solved.astype(jnp.float32)
```

```python
import functools
import heapq

import jax
import jax.numpy as jnp
from jax import lax
from jax.experimental import pallas as pl
from jax.experimental.pallas import tpu as pltpu
from jax.sharding import PartitionSpec as P

RW = 8
MOST = 32
WINDOW = MOST + 2
LAMBDA_REG = 1.0
NY, NZ = 4, 8
MESH = pl.DeviceIdType.MESH

PIECES = (
    ("y", 2, 1, 4, 3, 0, 7),
    ("y", 1, 2, 3, 4, 7, 6),
    ("z", 2, 1, 4, 3, 13, 9),
    ("z", 1, 2, 3, 4, 22, 10),
)
GROUP = 16


def children(piece, dy, dz):
    first, yp, ym, zp, zm = PIECES[piece][:5]
    out = []
    if (first == "y" and dz == 0) or first == "z":
        if 0 <= dy < yp:
            out.append((dy + 1, dz))
        if 0 >= dy > -ym:
            out.append((dy - 1, dz))
    if (first == "z" and dy == 0) or first == "y":
        if 0 <= dz < zp:
            out.append((dy, dz + 1))
        if 0 >= dz > -zm:
            out.append((dy, dz - 1))
    return out


def depth(piece, node):
    kids = children(piece, *node)
    return 1 + max(depth(piece, kid) for kid in kids) if kids else 0


def by_depth(piece, node):
    return sorted(children(piece, *node), key=lambda kid: -depth(piece, kid))


def order_of_arrival(lat=1.0, rate=0.164):
    free, heap, count = {}, [], 0

    def send(now, piece, par, kid):
        link = (kid[0] - par[0], kid[1] - par[1])
        free[link] = max(now, free.get(link, 0.0)) + PIECES[piece][6] * rate
        heapq.heappush(heap, (free[link] + lat, count, piece, kid))

    own = [(piece, kid) for piece in range(len(PIECES)) for kid in children(piece, 0, 0)]
    own.sort(key=lambda edge: -depth(*edge))
    for piece, kid in own:
        send(0.0, piece, (0, 0), kid)
        count += 1
    order = []
    while heap:
        now, _, piece, node = heapq.heappop(heap)
        order.append((piece, node))
        for kid in by_depth(piece, node):
            send(now, piece, node, kid)
            count += 1
    return own, order


def kernel(
    obs_hbm, firsts, rows_s, cols_s, fac_hbm, rhs_ref, gram_ref, fall, obs_v, obs_t, fac_t, win, eye, send_sem, recv_sem, loc_sem
):
    wide = lax.axis_index("wide")
    narrow = lax.axis_index("narrow")
    my_y, my_z = wide // NZ, wide % NZ
    own, order = order_of_arrival()
    number = {edge: at for at, edge in enumerate(order)}
    shard = fac_hbm.shape[0]
    slots = cols_s.shape[0]
    part = obs_hbm.shape[0] // slots
    width = obs_hbm.shape[1]
    rank = fac_hbm.shape[2]
    groups = part // GROUP
    nothing = (fall.shape[0] - groups) // groups
    lanes = 2 * part

    def device(dy, dz):
        return (((my_y + dy + NY) % NY) * NZ + (my_z + dz + NZ) % NZ, narrow)

    fac_copy = pltpu.make_async_copy(fac_hbm, fall.at[pl.ds(wide * shard, shard)], loc_sem.at[0])
    fac_copy.start()
    obs_copy = pltpu.make_async_copy(obs_hbm, obs_v, loc_sem.at[1])
    obs_copy.start()

    barrier = pltpu.get_barrier_semaphore()
    for step in ((1, 0), (-1, 0), (0, 1), (0, -1)):
        pl.semaphore_signal(barrier, inc=1, device_id=device(*step), device_id_type=MESH)
    fac_copy.wait()
    pl.semaphore_wait(barrier, 4)

    def place_of(piece, node):
        source = ((my_y - node[0] + NY) % NY) * NZ + (my_z - node[1] + NZ) % NZ
        return fall.at[pl.ds(source * shard + PIECES[piece][5], PIECES[piece][6])]

    def copy(piece, node, to, step):
        at = number[(piece, to)]
        place = place_of(piece, node)
        return pltpu.make_async_remote_copy(
            src_ref=place,
            dst_ref=place,
            send_sem=send_sem.at[at],
            recv_sem=recv_sem.at[at],
            device_id=device(*step),
            device_id_type=MESH,
        )

    sent = []

    def pass_on(piece, node, kid):
        sent.append(copy(piece, node, kid, (kid[0] - node[0], kid[1] - node[1])))
        sent[-1].start()

    for piece, kid in own:
        pass_on(piece, (0, 0), kid)

    down = lax.broadcasted_iota(jnp.int32, (rank, rank), 0)
    across = lax.broadcasted_iota(jnp.int32, (rank, rank), 1)
    eye[...] = jnp.where(down == across, 1.0, 0.0).astype(jnp.bfloat16)
    for t in range(groups):
        fall[nothing * groups + t] = jnp.zeros((GROUP, rank), jnp.bfloat16)

    def turned(tile):
        flat = lax.dot_general(eye[...], tile, (((1,), (1,)), ((), ())), preferred_element_type=jnp.float32)
        return flat.astype(jnp.bfloat16)

    def block(col):
        return jnp.concatenate([fall[col * groups + t] for t in range(groups)], axis=0)

    obs_copy.wait()
    wide_tiles = width // rank
    tiles = (slots * part // rank) * wide_tiles
    chunks = rank // lanes

    def turn_obs(tile):
        down_at, across_at = tile // wide_tiles, tile % wide_tiles
        flat = turned(obs_v[down_at * rank:(down_at + 1) * rank, across_at * rank:(across_at + 1) * rank])
        for t in range(chunks):
            obs_t[down_at * chunks + t, across_at * rank:(across_at + 1) * rank] = flat[:, t * lanes:(t + 1) * lanes]

    done = 0
    for at, (piece, node) in enumerate(order):
        copy(piece, node, node, (1, 0)).wait_recv()
        for kid in by_depth(piece, node):
            pass_on(piece, node, kid)
        while done < tiles and done * 100 < (at + 1) * tiles:
            turn_obs(done)
            done += 1

    @pl.loop(0, slots * part // rank)
    def turn_factors(step):
        few = rank // part
        flat = turned(jnp.concatenate([block(cols_s[step * few + t]) for t in range(few)], axis=0))
        for t in range(chunks):
            fac_t[step * chunks + t] = flat[:, t * lanes:(t + 1) * lanes]

    def window_of(ref, i):
        first = firsts[i]
        return jnp.concatenate([ref[first + t] for t in range(WINDOW // 2)], axis=1)

    @pl.loop(0, RW)
    def one_gram(i):
        first = firsts[i] * 2
        for t in range(WINDOW):
            col = jnp.where(rows_s[first + t] == i, cols_s[first + t], nothing)
            win[i, t * part:(t + 1) * part, :] = block(col)
        gram_ref[i] = jnp.dot(window_of(fac_t, i), win[i], preferred_element_type=jnp.float32)

    @pl.loop(0, RW)
    def one_rhs(i):
        rhs_ref[i] = jnp.dot(window_of(obs_t, i), win[i], preferred_element_type=jnp.float32)

    for out in sent:
        out.wait_send()


def partials(obs, rows, cols, factors):
    slots, part, width = obs.shape
    rank = factors.shape[-1]
    edges = len(order_of_arrival()[1])
    return pl.pallas_call(
        kernel,
        out_shape=(
            jax.ShapeDtypeStruct((RW, width, rank), jnp.float32),
            jax.ShapeDtypeStruct((RW, rank, rank), jnp.float32),
        ),
        in_specs=[
            pl.BlockSpec(memory_space=pl.ANY),
            pl.BlockSpec(memory_space=pltpu.SMEM),
            pl.BlockSpec(memory_space=pltpu.SMEM),
            pl.BlockSpec(memory_space=pltpu.SMEM),
            pl.BlockSpec(memory_space=pl.ANY),
        ],
        out_specs=(pl.BlockSpec(memory_space=pltpu.VMEM), pl.BlockSpec(memory_space=pltpu.VMEM)),
        scratch_shapes=[
            pltpu.VMEM(((NY * NZ * RW + 1) * part // GROUP, GROUP, rank), jnp.bfloat16),
            pltpu.VMEM((slots * part, width), jnp.bfloat16),
            pltpu.VMEM((slots // 2, width, 2 * part), jnp.bfloat16),
            pltpu.VMEM((slots // 2, rank, 2 * part), jnp.bfloat16),
            pltpu.VMEM((RW, WINDOW * part, rank), jnp.bfloat16),
            pltpu.VMEM((rank, rank), jnp.bfloat16),
            pltpu.SemaphoreType.DMA((edges,)),
            pltpu.SemaphoreType.DMA((edges,)),
            pltpu.SemaphoreType.DMA((2,)),
        ],
        compiler_params=pltpu.CompilerParams(collective_id=0, has_side_effects=True, vmem_limit_bytes=60 * 1024 * 1024),
        name="gather_and_multiply",
    )(
        obs.reshape(slots * part, width),
        window_starts(rows),
        rows,
        cols,
        factors.reshape(-1, GROUP, rank),
    )


def window_starts(rows):
    before = jnp.sum((rows[None, :] < jnp.arange(RW, dtype=jnp.int32)[:, None]).astype(jnp.int32), axis=1)
    return jnp.minimum(before // 2, (rows.shape[0] - WINDOW) // 2)


def solve_rows(rhs, gram):
    chol = jnp.linalg.cholesky(gram)
    forward = lax.linalg.triangular_solve(chol, rhs, left_side=False, lower=True, transpose_a=True)
    return lax.linalg.triangular_solve(
        chol, forward, left_side=False, lower=True, transpose_a=False
    )


def body(obs_blocks, obs_row, obs_col, factors):
    rank = factors.shape[2]
    rhs_part, gram_part = partials(obs_blocks[0], obs_row[0], obs_col[0], factors)
    identity = jnp.eye(rank, dtype=jnp.float32)[None]
    rhs_total = lax.psum_scatter(rhs_part, "narrow", scatter_dimension=0, tiled=True)
    gram_total = lax.psum_scatter(gram_part, "narrow", scatter_dimension=0, tiled=True)
    return solve_rows(rhs_total, gram_total + LAMBDA_REG * identity)


def solution(mesh):
    placed = (
        P("wide", None, "narrow", None),
        P("wide", None),
        P("wide", None),
        P("wide", "narrow", None),
    )
    return jax.shard_map(
        body,
        mesh=mesh,
        in_specs=placed,
        out_specs=P(("wide", "narrow"), None, None),
        check_vma=False,
    )
```

```python
import functools
import heapq

import jax
import jax.numpy as jnp
from jax import lax
from jax.experimental import pallas as pl
from jax.experimental.pallas import tpu as pltpu
from jax.sharding import PartitionSpec as P

RW = 8
MOST = 32
WINDOW = MOST + 2
LAMBDA_REG = 1.0
NX, NY, NZ = 4, 4, 8
MESH = pl.DeviceIdType.MESH

PIECES = (
    ("y", 2, 1, 4, 3, 0, 7),
    ("y", 1, 2, 3, 4, 7, 6),
    ("z", 2, 1, 4, 3, 13, 9),
    ("z", 1, 2, 3, 4, 22, 10),
)
GROUP = 16
PANEL = 32


def children(piece, dy, dz):
    first, yp, ym, zp, zm = PIECES[piece][:5]
    out = []
    if (first == "y" and dz == 0) or first == "z":
        if 0 <= dy < yp:
            out.append((dy + 1, dz))
        if 0 >= dy > -ym:
            out.append((dy - 1, dz))
    if (first == "z" and dy == 0) or first == "y":
        if 0 <= dz < zp:
            out.append((dy, dz + 1))
        if 0 >= dz > -zm:
            out.append((dy, dz - 1))
    return out


def depth(piece, node):
    kids = children(piece, *node)
    return 1 + max(depth(piece, kid) for kid in kids) if kids else 0


def by_depth(piece, node):
    return sorted(children(piece, *node), key=lambda kid: -depth(piece, kid))


def order_of_arrival(lat=1.0, rate=0.164):
    free, heap, count = {}, [], 0

    def send(now, piece, par, kid):
        link = (kid[0] - par[0], kid[1] - par[1])
        free[link] = max(now, free.get(link, 0.0)) + PIECES[piece][6] * rate
        heapq.heappush(heap, (free[link] + lat, count, piece, kid))

    own = [(piece, kid) for piece in range(len(PIECES)) for kid in children(piece, 0, 0)]
    own.sort(key=lambda edge: -depth(*edge))
    for piece, kid in own:
        send(0.0, piece, (0, 0), kid)
        count += 1
    order = []
    while heap:
        now, _, piece, node = heapq.heappop(heap)
        order.append((piece, node))
        for kid in by_depth(piece, node):
            send(now, piece, node, kid)
            count += 1
    return own, order


class RowSum:
    def __init__(self, rows, pair, ring, send_sem, recv_sem, base, my_x, my_core, beside):
        self.rows, self.pair, self.ring = rows, pair, ring
        self.send_sem, self.recv_sem, self.base = send_sem, recv_sem, base
        self.my_x, self.my_core, self.beside = my_x, my_core, beside
        self.half = rows.shape[1] // 2
        self.sent = []

    def chip(self, ahead):
        return (self.my_x + ahead + NX) % NX

    def row(self, ahead, other):
        return self.chip(ahead) * 2 + (1 - self.my_core if other else self.my_core)

    def near(self, ahead, q):
        return pltpu.make_async_remote_copy(
            src_ref=self.rows.at[self.row(ahead, True)],
            dst_ref=self.pair.at[self.chip(ahead)],
            send_sem=self.send_sem.at[self.base + q],
            recv_sem=self.recv_sem.at[self.base + q],
            device_id=self.beside(0, 1),
            device_id_type=MESH,
        )

    def hop(self, slot, ahead, upper, step):
        at = self.base + 4 + slot
        return pltpu.make_async_remote_copy(
            src_ref=self.rows.at[self.row(ahead, False), pl.ds(self.half if upper else 0, self.half)],
            dst_ref=self.ring.at[slot],
            send_sem=self.send_sem.at[at],
            recv_sem=self.recv_sem.at[at],
            device_id=self.beside(step, 0),
            device_id_type=MESH,
        )

    def start(self, *what):
        self.sent.append(self.hop(*what))
        self.sent[-1].start()

    def arrived(self, slot):
        self.hop(slot, 1, False, 1).wait_recv()

    def fold(self, q):
        ahead = (2 - q + NX) % NX
        self.near(ahead, q).wait_recv()
        mine = self.row(ahead, False)
        self.rows[mine] = self.rows[mine] + self.pair[self.chip(ahead)]
        if ahead == 2:
            self.start(0, 2, False, 1)
            self.start(1, 2, True, -1)
        elif ahead == 1:
            self.start(2, 1, True, 1)
        elif ahead == 3:
            self.start(3, 3, False, -1)

    def forward(self):
        half = self.half
        self.arrived(0)
        up = self.row(1, False)
        self.rows[up, 0:half] = self.rows[up, 0:half] + self.ring[0]
        self.start(4, 1, False, 1)
        self.arrived(1)
        back = self.row(3, False)
        self.rows[back, half:2 * half] = self.rows[back, half:2 * half] + self.ring[1]
        self.start(5, 3, True, -1)

    def total(self):
        for slot in (2, 3, 4, 5):
            self.arrived(slot)
        mine, half = self.row(0, False), self.half
        low = self.rows[mine, 0:half] + self.ring[4] + self.ring[3]
        high = self.rows[mine, half:2 * half] + self.ring[5] + self.ring[2]
        return low, high

    def finish(self):
        for q in range(NX):
            self.near((2 - q + NX) % NX, q).wait_send()
        for out in self.sent:
            out.wait_send()


def small_inverse(block):
    size = block.shape[0]
    down = lax.broadcasted_iota(jnp.int32, (size, size), 0)
    across = lax.broadcasted_iota(jnp.int32, (size, size), 1)
    for j in range(size):
        pivot = 1.0 / block[j:j + 1, j:j + 1]
        row = jnp.where(across[j:j + 1] == j, pivot, block[j:j + 1] * pivot)
        col = block[:, j:j + 1]
        block = jnp.where(down == j, row, jnp.where(across == j, 0.0, block) - col * row)
    return block


def eliminate(inv, low, high):
    pivot = small_inverse(inv[low:high, low:high])
    rows = jnp.dot(pivot, inv[low:high, :], precision=lax.Precision.HIGHEST, preferred_element_type=jnp.float32)
    cols = inv[:, low:high]
    change = jnp.dot(cols, rows, precision=lax.Precision.HIGHEST, preferred_element_type=jnp.float32)
    side = jnp.dot(cols, pivot, precision=lax.Precision.HIGHEST, preferred_element_type=jnp.float32)
    inv[...] = inv[...] - change
    inv[:, low:high] = -side
    inv[low:high, :] = rows
    inv[low:high, low:high] = pivot


def kernel(
    obs_hbm, firsts, rows_s, cols_s, fac_hbm, out_ref, fall, obs_v, obs_t, fac_t, win, eye,
    gram, gram_near, gram_ring, rhs, rhs_near, rhs_ring, inv, send_sem, recv_sem, loc_sem, sum_send, sum_recv
):
    wide = lax.axis_index("wide")
    narrow = lax.axis_index("narrow")
    my_y, my_z = wide // NZ, wide % NZ
    own, order = order_of_arrival()
    number = {edge: at for at, edge in enumerate(order)}
    shard = fac_hbm.shape[0]
    slots = cols_s.shape[0]
    part = obs_hbm.shape[0] // slots
    width = obs_hbm.shape[1]
    rank = fac_hbm.shape[2]
    groups = part // GROUP
    nothing = (fall.shape[0] - groups) // groups
    lanes = 2 * part

    def device(dy, dz):
        return (((my_y + dy + NY) % NY) * NZ + (my_z + dz + NZ) % NZ, narrow)

    my_x, my_core = narrow // 2, narrow % 2

    def beside(dx, other):
        core = 1 - my_core if other else my_core
        return (wide, (my_x + dx + NX) % NX * 2 + core)

    fac_copy = pltpu.make_async_copy(fac_hbm, fall.at[pl.ds(wide * shard, shard)], loc_sem.at[0])
    fac_copy.start()
    obs_copy = pltpu.make_async_copy(obs_hbm, obs_v, loc_sem.at[1])
    obs_copy.start()

    barrier = pltpu.get_barrier_semaphore()
    partners = [device(*step) for step in ((1, 0), (-1, 0), (0, 1), (0, -1))]
    partners += [beside(0, 1), beside(1, 0), beside(-1, 0)]
    for partner in partners:
        pl.semaphore_signal(barrier, inc=1, device_id=partner, device_id_type=MESH)
    fac_copy.wait()
    pl.semaphore_wait(barrier, len(partners))

    def place_of(piece, node):
        source = ((my_y - node[0] + NY) % NY) * NZ + (my_z - node[1] + NZ) % NZ
        return fall.at[pl.ds(source * shard + PIECES[piece][5], PIECES[piece][6])]

    def copy(piece, node, to, step):
        at = number[(piece, to)]
        place = place_of(piece, node)
        return pltpu.make_async_remote_copy(
            src_ref=place,
            dst_ref=place,
            send_sem=send_sem.at[at],
            recv_sem=recv_sem.at[at],
            device_id=device(*step),
            device_id_type=MESH,
        )

    sent = []

    def pass_on(piece, node, kid):
        sent.append(copy(piece, node, kid, (kid[0] - node[0], kid[1] - node[1])))
        sent[-1].start()

    for piece, kid in own:
        pass_on(piece, (0, 0), kid)

    down = lax.broadcasted_iota(jnp.int32, (rank, rank), 0)
    across = lax.broadcasted_iota(jnp.int32, (rank, rank), 1)
    eye[...] = jnp.where(down == across, 1.0, 0.0).astype(jnp.bfloat16)
    for t in range(groups):
        fall[nothing * groups + t] = jnp.zeros((GROUP, rank), jnp.bfloat16)

    def turned(tile):
        flat = lax.dot_general(eye[...], tile, (((1,), (1,)), ((), ())), preferred_element_type=jnp.float32)
        return flat.astype(jnp.bfloat16)

    def block(col):
        return jnp.concatenate([fall[col * groups + t] for t in range(groups)], axis=0)

    obs_copy.wait()
    wide_tiles = width // rank
    tiles = (slots * part // rank) * wide_tiles
    chunks = rank // lanes

    def turn_obs(tile):
        down_at, across_at = tile // wide_tiles, tile % wide_tiles
        flat = turned(obs_v[down_at * rank:(down_at + 1) * rank, across_at * rank:(across_at + 1) * rank])
        for t in range(chunks):
            obs_t[down_at * chunks + t, across_at * rank:(across_at + 1) * rank] = flat[:, t * lanes:(t + 1) * lanes]

    done = 0
    for at, (piece, node) in enumerate(order):
        copy(piece, node, node, (1, 0)).wait_recv()
        for kid in by_depth(piece, node):
            pass_on(piece, node, kid)
        while done < tiles and done * 100 < (at + 1) * tiles:
            turn_obs(done)
            done += 1

    @pl.loop(0, slots * part // rank)
    def turn_factors(step):
        few = rank // part
        flat = turned(jnp.concatenate([block(cols_s[step * few + t]) for t in range(few)], axis=0))
        for t in range(chunks):
            fac_t[step * chunks + t] = flat[:, t * lanes:(t + 1) * lanes]

    def window_of(ref, i):
        first = firsts[i]
        return jnp.concatenate([ref[first + t] for t in range(WINDOW // 2)], axis=1)

    gram_sum = RowSum(gram, gram_near, gram_ring, sum_send, sum_recv, 0, my_x, my_core, beside)
    rhs_sum = RowSum(rhs, rhs_near, rhs_ring, sum_send, sum_recv, 10, my_x, my_core, beside)
    half = rank // 2

    def gram_of(row):
        first = firsts[row] * 2
        for t in range(WINDOW):
            col = jnp.where(rows_s[first + t] == row, cols_s[first + t], nothing)
            win[row, t * part:(t + 1) * part, :] = block(col)
        whole = jnp.dot(window_of(fac_t, row), win[row], preferred_element_type=jnp.float32)
        gram[row, 0:rank, :] = whole[:, :half]
        gram[row, rank:rank + half, :] = whole[half:, half:]

    def rhs_of(row):
        rhs[row] = jnp.dot(window_of(obs_t, row), win[row], preferred_element_type=jnp.float32)

    @pl.loop(0, NX)
    def grams(q):
        ahead = (2 - q + NX) % NX
        gram_of(gram_sum.row(ahead, True))
        gram_sum.near(ahead, q).start()
        gram_of(gram_sum.row(ahead, False))

    def rhs_pair(q):
        ahead = (2 - q + NX) % NX
        rhs_of(rhs_sum.row(ahead, True))
        rhs_sum.near(ahead, q).start()
        rhs_of(rhs_sum.row(ahead, False))

    for q in range(NX):
        gram_sum.fold(q)
    pl.loop(0, 2)(rhs_pair)
    gram_sum.forward()
    rhs_sum.fold(0)
    rhs_sum.fold(1)
    pl.loop(2, NX)(rhs_pair)
    rhs_sum.fold(2)
    rhs_sum.fold(3)

    low, high = gram_sum.total()
    packed = jnp.concatenate([low, high], axis=0)
    same = jnp.where(down == across, LAMBDA_REG, 0.0)
    inv[:half, :half] = packed[:half] + same[:half, :half]
    inv[half:, :half] = packed[half:rank]
    inv[:half, half:] = packed[half:rank].T
    inv[half:, half:] = packed[rank:] + same[:half, :half]

    panels = rank // PANEL
    for p in range(panels):
        if p == panels // 2:
            rhs_sum.forward()
        eliminate(inv, p * PANEL, (p + 1) * PANEL)

    low, high = rhs_sum.total()
    out_ref[0:width // 2] = jnp.dot(low, inv[...], precision=lax.Precision.HIGHEST, preferred_element_type=jnp.float32)
    out_ref[width // 2:] = jnp.dot(high, inv[...], precision=lax.Precision.HIGHEST, preferred_element_type=jnp.float32)

    gram_sum.finish()
    rhs_sum.finish()
    for out in sent:
        out.wait_send()


def solved_row(obs, rows, cols, factors):
    slots, part, width = obs.shape
    rank = factors.shape[-1]
    edges = len(order_of_arrival()[1])
    return pl.pallas_call(
        kernel,
        out_shape=jax.ShapeDtypeStruct((width, rank), jnp.float32),
        in_specs=[
            pl.BlockSpec(memory_space=pl.ANY),
            pl.BlockSpec(memory_space=pltpu.SMEM),
            pl.BlockSpec(memory_space=pltpu.SMEM),
            pl.BlockSpec(memory_space=pltpu.SMEM),
            pl.BlockSpec(memory_space=pl.ANY),
        ],
        out_specs=pl.BlockSpec(memory_space=pltpu.VMEM),
        scratch_shapes=[
            pltpu.VMEM(((NY * NZ * RW + 1) * part // GROUP, GROUP, rank), jnp.bfloat16),
            pltpu.VMEM((slots * part, width), jnp.bfloat16),
            pltpu.VMEM((slots // 2, width, 2 * part), jnp.bfloat16),
            pltpu.VMEM((slots // 2, rank, 2 * part), jnp.bfloat16),
            pltpu.VMEM((RW, WINDOW * part, rank), jnp.bfloat16),
            pltpu.VMEM((rank, rank), jnp.bfloat16),
            pltpu.VMEM((RW, rank + rank // 2, rank // 2), jnp.float32),
            pltpu.VMEM((NX, rank + rank // 2, rank // 2), jnp.float32),
            pltpu.VMEM((6, (rank + rank // 2) // 2, rank // 2), jnp.float32),
            pltpu.VMEM((RW, width, rank), jnp.float32),
            pltpu.VMEM((NX, width, rank), jnp.float32),
            pltpu.VMEM((6, width // 2, rank), jnp.float32),
            pltpu.VMEM((rank, rank), jnp.float32),
            pltpu.SemaphoreType.DMA((edges,)),
            pltpu.SemaphoreType.DMA((edges,)),
            pltpu.SemaphoreType.DMA((2,)),
            pltpu.SemaphoreType.DMA((20,)),
            pltpu.SemaphoreType.DMA((20,)),
        ],
        compiler_params=pltpu.CompilerParams(collective_id=0, has_side_effects=True, vmem_limit_bytes=60 * 1024 * 1024),
        name="solve_rows",
    )(
        obs.reshape(slots * part, width),
        window_starts(rows),
        rows,
        cols,
        factors.reshape(-1, GROUP, rank),
    )


def window_starts(rows):
    before = jnp.sum((rows[None, :] < jnp.arange(RW, dtype=jnp.int32)[:, None]).astype(jnp.int32), axis=1)
    return jnp.minimum(before // 2, (rows.shape[0] - WINDOW) // 2)


def body(obs_blocks, obs_row, obs_col, factors):
    return solved_row(obs_blocks[0], obs_row[0], obs_col[0], factors)[None]


def solution(mesh):
    placed = (
        P("wide", None, "narrow", None),
        P("wide", None),
        P("wide", None),
        P("wide", "narrow", None),
    )
    return jax.shard_map(
        body,
        mesh=mesh,
        in_specs=placed,
        out_specs=P(("wide", "narrow"), None, None),
        check_vma=False,
    )
```

```python
import functools
import heapq

import jax
import jax.numpy as jnp
from jax import lax
from jax.experimental import pallas as pl
from jax.experimental.pallas import tpu as pltpu
from jax.sharding import PartitionSpec as P

RW = 8
MOST = 32
WINDOW = MOST + 2
LAMBDA_REG = 1.0
NX, NY, NZ = 4, 4, 8
MESH = pl.DeviceIdType.MESH

PIECES = (
    ("y", 2, 1, 4, 3, 0, 7),
    ("y", 1, 2, 3, 4, 7, 6),
    ("z", 2, 1, 4, 3, 13, 9),
    ("z", 1, 2, 3, 4, 22, 10),
)
GROUP = 16
PANEL = 64


def children(piece, dy, dz):
    first, yp, ym, zp, zm = PIECES[piece][:5]
    out = []
    if (first == "y" and dz == 0) or first == "z":
        if 0 <= dy < yp:
            out.append((dy + 1, dz))
        if 0 >= dy > -ym:
            out.append((dy - 1, dz))
    if (first == "z" and dy == 0) or first == "y":
        if 0 <= dz < zp:
            out.append((dy, dz + 1))
        if 0 >= dz > -zm:
            out.append((dy, dz - 1))
    return out


def depth(piece, node):
    kids = children(piece, *node)
    return 1 + max(depth(piece, kid) for kid in kids) if kids else 0


def by_depth(piece, node):
    return sorted(children(piece, *node), key=lambda kid: -depth(piece, kid))


def order_of_arrival(lat=1.0, rate=0.164):
    free, heap, count = {}, [], 0

    def send(now, piece, par, kid):
        link = (kid[0] - par[0], kid[1] - par[1])
        free[link] = max(now, free.get(link, 0.0)) + PIECES[piece][6] * rate
        heapq.heappush(heap, (free[link] + lat, count, piece, kid))

    own = [(piece, kid) for piece in range(len(PIECES)) for kid in children(piece, 0, 0)]
    own.sort(key=lambda edge: -depth(*edge))
    for piece, kid in own:
        send(0.0, piece, (0, 0), kid)
        count += 1
    order = []
    while heap:
        now, _, piece, node = heapq.heappop(heap)
        order.append((piece, node))
        for kid in by_depth(piece, node):
            send(now, piece, node, kid)
            count += 1
    return own, order


class RowSum:
    def __init__(self, rows, pair, ring, send_sem, recv_sem, base, my_x, my_core, beside):
        self.rows, self.pair, self.ring = rows, pair, ring
        self.send_sem, self.recv_sem, self.base = send_sem, recv_sem, base
        self.my_x, self.my_core, self.beside = my_x, my_core, beside
        self.half = rows.shape[1] // 2
        self.sent = []

    def chip(self, ahead):
        return (self.my_x + ahead + NX) % NX

    def row(self, ahead, other):
        return self.chip(ahead) * 2 + (1 - self.my_core if other else self.my_core)

    def near(self, ahead, q):
        return pltpu.make_async_remote_copy(
            src_ref=self.rows.at[self.row(ahead, True)],
            dst_ref=self.pair.at[self.chip(ahead)],
            send_sem=self.send_sem.at[self.base + q],
            recv_sem=self.recv_sem.at[self.base + q],
            device_id=self.beside(0, 1),
            device_id_type=MESH,
        )

    def hop(self, slot, ahead, upper, step):
        at = self.base + 4 + slot
        return pltpu.make_async_remote_copy(
            src_ref=self.rows.at[self.row(ahead, False), pl.ds(self.half if upper else 0, self.half)],
            dst_ref=self.ring.at[slot],
            send_sem=self.send_sem.at[at],
            recv_sem=self.recv_sem.at[at],
            device_id=self.beside(step, 0),
            device_id_type=MESH,
        )

    def start(self, *what):
        self.sent.append(self.hop(*what))
        self.sent[-1].start()

    def arrived(self, slot):
        self.hop(slot, 1, False, 1).wait_recv()

    def fold(self, q):
        ahead = (2 - q + NX) % NX
        self.near(ahead, q).wait_recv()
        mine = self.row(ahead, False)
        self.rows[mine] = self.rows[mine] + self.pair[self.chip(ahead)]
        if ahead == 2:
            self.start(0, 2, False, 1)
            self.start(1, 2, True, -1)
        elif ahead == 1:
            self.start(2, 1, True, 1)
        elif ahead == 3:
            self.start(3, 3, False, -1)

    def forward(self):
        half = self.half
        self.arrived(0)
        up = self.row(1, False)
        self.rows[up, 0:half] = self.rows[up, 0:half] + self.ring[0]
        self.start(4, 1, False, 1)
        self.arrived(1)
        back = self.row(3, False)
        self.rows[back, half:2 * half] = self.rows[back, half:2 * half] + self.ring[1]
        self.start(5, 3, True, -1)

    def total(self):
        for slot in (2, 3, 4, 5):
            self.arrived(slot)
        mine, half = self.row(0, False), self.half
        low = self.rows[mine, 0:half] + self.ring[4] + self.ring[3]
        high = self.rows[mine, half:2 * half] + self.ring[5] + self.ring[2]
        return low, high

    def finish(self):
        for q in range(NX):
            self.near((2 - q + NX) % NX, q).wait_send()
        for out in self.sent:
            out.wait_send()


def inverse_2x2(a, b, c):
    scale = 1.0 / (a * c - b * b)
    return c * scale, -b * scale, a * scale


def inverse_4x4(m):
    a, b, c = inverse_2x2(m[0][0], m[0][1], m[1][1])
    top = [[a * m[0][k] + b * m[1][k] for k in (2, 3)], [b * m[0][k] + c * m[1][k] for k in (2, 3)]]

    def rest(k, l):
        return m[k][l] - (m[0][k] * top[0][l - 2] + m[1][k] * top[1][l - 2])

    p, q, r = inverse_2x2(rest(2, 2), rest(2, 3), rest(3, 3))
    side = [[-(top[k][0] * p + top[k][1] * q), -(top[k][0] * q + top[k][1] * r)] for k in (0, 1)]
    aa = a - (side[0][0] * top[0][0] + side[0][1] * top[0][1])
    bb = b - (side[0][0] * top[1][0] + side[0][1] * top[1][1])
    cc = c - (side[1][0] * top[1][0] + side[1][1] * top[1][1])
    return [
        [aa, bb, side[0][0], side[0][1]],
        [bb, cc, side[1][0], side[1][1]],
        [side[0][0], side[1][0], p, q],
        [side[0][1], side[1][1], q, r],
    ]


def small_inverse(block):
    size = block.shape[0]
    down = lax.broadcasted_iota(jnp.int32, (size, size), 0)
    across = lax.broadcasted_iota(jnp.int32, (size, size), 1)
    lane = across[0:8]
    for j in range(0, size, 4):
        cols = [jnp.broadcast_to(block[:, j + k:j + k + 1], (size, size)) for k in range(4)]
        rows = [jnp.broadcast_to(block[j + k:j + k + 1], (8, size)) for k in range(4)]
        pivot = [[jnp.broadcast_to(cols[max(k, l)][j + min(k, l):j + min(k, l) + 1], (8, size)) for l in range(4)] for k in range(4)]
        inverse = inverse_4x4(pivot)
        rest = jnp.where((across >= j) & (across < j + 4), 0.0, block)
        done = []
        for k in range(4):
            row = (inverse[k][0] * rows[0] + inverse[k][1] * rows[1]) + (inverse[k][2] * rows[2] + inverse[k][3] * rows[3])
            for l in range(4):
                row = jnp.where(lane == j + l, inverse[k][l], row)
            done.append(jnp.concatenate([row] * (size // 8), axis=0))
        rest = rest - ((cols[0] * done[0] + cols[1] * done[1]) + (cols[2] * done[2] + cols[3] * done[3]))
        for k in range(4):
            rest = jnp.where(down == j + k, done[k], rest)
        block = rest
    return block


def exact_dot(x, y):
    return jnp.dot(x, y, precision=lax.Precision.HIGHEST, preferred_element_type=jnp.float32)


def eliminate(inv, low, high):
    pivot = small_inverse(inv[low:high, low:high])
    inv[low:high, :] = exact_dot(pivot, inv[low:high, :])
    inv[low:high, low:high] = pivot
    rows = inv[low:high, :]
    for part in ((0, low), (high, inv.shape[0])):
        if part[0] < part[1]:
            cols = inv[part[0]:part[1], low:high]
            inv[part[0]:part[1], low:high] = jnp.zeros_like(cols)
            inv[part[0]:part[1], :] = inv[part[0]:part[1], :] - exact_dot(cols, rows)


def kernel(
    obs_hbm, firsts, rows_s, cols_s, fac_hbm, out_ref, fall, obs_v, obs_t, fac_t, win, eye,
    gram, gram_near, gram_ring, rhs, rhs_near, rhs_ring, inv, whole_gram, send_sem, recv_sem, loc_sem, sum_send, sum_recv
):
    wide = lax.axis_index("wide")
    narrow = lax.axis_index("narrow")
    my_y, my_z = wide // NZ, wide % NZ
    own, order = order_of_arrival()
    number = {edge: at for at, edge in enumerate(order)}
    shard = fac_hbm.shape[0]
    slots = cols_s.shape[0]
    part = obs_hbm.shape[0] // slots
    width = obs_hbm.shape[1]
    rank = fac_hbm.shape[2]
    groups = part // GROUP
    nothing = (fall.shape[0] - groups) // groups
    lanes = 2 * part

    def device(dy, dz):
        return (((my_y + dy + NY) % NY) * NZ + (my_z + dz + NZ) % NZ, narrow)

    my_x, my_core = narrow // 2, narrow % 2

    def beside(dx, other):
        core = 1 - my_core if other else my_core
        return (wide, (my_x + dx + NX) % NX * 2 + core)

    fac_copy = pltpu.make_async_copy(fac_hbm, fall.at[pl.ds(wide * shard, shard)], loc_sem.at[0])
    fac_copy.start()
    obs_copy = pltpu.make_async_copy(obs_hbm, obs_v, loc_sem.at[1])
    obs_copy.start()

    barrier = pltpu.get_barrier_semaphore()
    partners = [device(*step) for step in ((1, 0), (-1, 0), (0, 1), (0, -1))]
    partners += [beside(0, 1), beside(1, 0), beside(-1, 0)]
    for partner in partners:
        pl.semaphore_signal(barrier, inc=1, device_id=partner, device_id_type=MESH)
    fac_copy.wait()
    pl.semaphore_wait(barrier, len(partners))

    def place_of(piece, node):
        source = ((my_y - node[0] + NY) % NY) * NZ + (my_z - node[1] + NZ) % NZ
        return fall.at[pl.ds(source * shard + PIECES[piece][5], PIECES[piece][6])]

    def copy(piece, node, to, step):
        at = number[(piece, to)]
        place = place_of(piece, node)
        return pltpu.make_async_remote_copy(
            src_ref=place,
            dst_ref=place,
            send_sem=send_sem.at[at],
            recv_sem=recv_sem.at[at],
            device_id=device(*step),
            device_id_type=MESH,
        )

    sent = []

    def pass_on(piece, node, kid):
        sent.append(copy(piece, node, kid, (kid[0] - node[0], kid[1] - node[1])))
        sent[-1].start()

    for piece, kid in own:
        pass_on(piece, (0, 0), kid)

    down = lax.broadcasted_iota(jnp.int32, (rank, rank), 0)
    across = lax.broadcasted_iota(jnp.int32, (rank, rank), 1)
    eye[...] = jnp.where(down == across, 1.0, 0.0).astype(jnp.bfloat16)
    for t in range(groups):
        fall[nothing * groups + t] = jnp.zeros((GROUP, rank), jnp.bfloat16)

    def turned(tile):
        flat = lax.dot_general(eye[...], tile, (((1,), (1,)), ((), ())), preferred_element_type=jnp.float32)
        return flat.astype(jnp.bfloat16)

    def block(col):
        return jnp.concatenate([fall[col * groups + t] for t in range(groups)], axis=0)

    obs_copy.wait()
    wide_tiles = width // rank
    tiles = (slots * part // rank) * wide_tiles
    chunks = rank // lanes

    def turn_obs(tile):
        down_at, across_at = tile // wide_tiles, tile % wide_tiles
        flat = turned(obs_v[down_at * rank:(down_at + 1) * rank, across_at * rank:(across_at + 1) * rank])
        for t in range(chunks):
            obs_t[down_at * chunks + t, across_at * rank:(across_at + 1) * rank] = flat[:, t * lanes:(t + 1) * lanes]

    done = 0
    for at, (piece, node) in enumerate(order):
        copy(piece, node, node, (1, 0)).wait_recv()
        for kid in by_depth(piece, node):
            pass_on(piece, node, kid)
        while done < tiles and done * 100 < (at + 1) * tiles:
            turn_obs(done)
            done += 1

    @pl.loop(0, slots * part // rank)
    def turn_factors(step):
        few = rank // part
        flat = turned(jnp.concatenate([block(cols_s[step * few + t]) for t in range(few)], axis=0))
        for t in range(chunks):
            fac_t[step * chunks + t] = flat[:, t * lanes:(t + 1) * lanes]

    def window_of(ref, i):
        first = firsts[i]
        return jnp.concatenate([ref[first + t] for t in range(WINDOW // 2)], axis=1)

    gram_sum = RowSum(gram, gram_near, gram_ring, sum_send, sum_recv, 0, my_x, my_core, beside)
    rhs_sum = RowSum(rhs, rhs_near, rhs_ring, sum_send, sum_recv, 10, my_x, my_core, beside)
    half = rank // 2

    def gram_of(row):
        first = firsts[row] * 2
        for t in range(WINDOW):
            col = jnp.where(rows_s[first + t] == row, cols_s[first + t], nothing)
            win[row, t * part:(t + 1) * part, :] = block(col)
        whole = jnp.dot(window_of(fac_t, row), win[row], preferred_element_type=jnp.float32)
        gram[row, 0:rank, :] = whole[:, :half]
        gram[row, rank:rank + half, :] = whole[half:, half:]

    def rhs_of(row):
        rhs[row] = jnp.dot(window_of(obs_t, row), win[row], preferred_element_type=jnp.float32)

    @pl.loop(0, NX)
    def grams(q):
        ahead = (2 - q + NX) % NX
        gram_of(gram_sum.row(ahead, True))
        gram_sum.near(ahead, q).start()
        gram_of(gram_sum.row(ahead, False))

    def rhs_pair(q):
        ahead = (2 - q + NX) % NX
        rhs_of(rhs_sum.row(ahead, True))
        rhs_sum.near(ahead, q).start()
        rhs_of(rhs_sum.row(ahead, False))

    for q in range(NX):
        gram_sum.fold(q)
    pl.loop(0, 2)(rhs_pair)
    gram_sum.forward()
    rhs_sum.fold(0)
    rhs_sum.fold(1)
    pl.loop(2, NX)(rhs_pair)
    rhs_sum.fold(2)
    rhs_sum.fold(3)

    low, high = gram_sum.total()
    packed = jnp.concatenate([low, high], axis=0)
    same = jnp.where(down == across, LAMBDA_REG, 0.0)
    inv[:half, :half] = packed[:half] + same[:half, :half]
    inv[half:, :half] = packed[half:rank]
    inv[:half, half:] = packed[half:rank].T
    inv[half:, half:] = packed[rank:] + same[:half, :half]

    whole_gram[...] = inv[...]
    panels = rank // PANEL
    for p in range(panels):
        if p == panels // 2:
            rhs_sum.forward()
        eliminate(inv, p * PANEL, (p + 1) * PANEL)

    for part_of, total in enumerate(rhs_sum.total()):
        at = slice(part_of * (width // 2), (part_of + 1) * (width // 2))
        first = exact_dot(total, inv[...])
        out_ref[at] = first + exact_dot(total - exact_dot(first, whole_gram[...]), inv[...])

    gram_sum.finish()
    rhs_sum.finish()
    for out in sent:
        out.wait_send()


def solved_row(obs, rows, cols, factors):
    slots, part, width = obs.shape
    rank = factors.shape[-1]
    edges = len(order_of_arrival()[1])
    return pl.pallas_call(
        kernel,
        out_shape=jax.ShapeDtypeStruct((width, rank), jnp.float32),
        in_specs=[
            pl.BlockSpec(memory_space=pl.ANY),
            pl.BlockSpec(memory_space=pltpu.SMEM),
            pl.BlockSpec(memory_space=pltpu.SMEM),
            pl.BlockSpec(memory_space=pltpu.SMEM),
            pl.BlockSpec(memory_space=pl.ANY),
        ],
        out_specs=pl.BlockSpec(memory_space=pltpu.VMEM),
        scratch_shapes=[
            pltpu.VMEM(((NY * NZ * RW + 1) * part // GROUP, GROUP, rank), jnp.bfloat16),
            pltpu.VMEM((slots * part, width), jnp.bfloat16),
            pltpu.VMEM((slots // 2, width, 2 * part), jnp.bfloat16),
            pltpu.VMEM((slots // 2, rank, 2 * part), jnp.bfloat16),
            pltpu.VMEM((RW, WINDOW * part, rank), jnp.bfloat16),
            pltpu.VMEM((rank, rank), jnp.bfloat16),
            pltpu.VMEM((RW, rank + rank // 2, rank // 2), jnp.float32),
            pltpu.VMEM((NX, rank + rank // 2, rank // 2), jnp.float32),
            pltpu.VMEM((6, (rank + rank // 2) // 2, rank // 2), jnp.float32),
            pltpu.VMEM((RW, width, rank), jnp.float32),
            pltpu.VMEM((NX, width, rank), jnp.float32),
            pltpu.VMEM((6, width // 2, rank), jnp.float32),
            pltpu.VMEM((rank, rank), jnp.float32),
            pltpu.VMEM((rank, rank), jnp.float32),
            pltpu.SemaphoreType.DMA((edges,)),
            pltpu.SemaphoreType.DMA((edges,)),
            pltpu.SemaphoreType.DMA((2,)),
            pltpu.SemaphoreType.DMA((20,)),
            pltpu.SemaphoreType.DMA((20,)),
        ],
        compiler_params=pltpu.CompilerParams(collective_id=0, has_side_effects=True, vmem_limit_bytes=60 * 1024 * 1024),
        name="solve_rows",
    )(
        obs.reshape(slots * part, width),
        window_starts(rows),
        rows,
        cols,
        factors.reshape(-1, GROUP, rank),
    )


def window_starts(rows):
    before = jnp.sum((rows[None, :] < jnp.arange(RW, dtype=jnp.int32)[:, None]).astype(jnp.int32), axis=1)
    return jnp.minimum(before // 2, (rows.shape[0] - WINDOW) // 2)


def body(obs_blocks, obs_row, obs_col, factors):
    return solved_row(obs_blocks[0], obs_row[0], obs_col[0], factors)[None]


def solution(mesh):
    placed = (
        P("wide", None, "narrow", None),
        P("wide", None),
        P("wide", None),
        P("wide", "narrow", None),
    )
    return jax.shard_map(
        body,
        mesh=mesh,
        in_specs=placed,
        out_specs=P(("wide", "narrow"), None, None),
        check_vma=False,
    )
```

```python
import functools
import heapq

import jax
import jax.numpy as jnp
from jax import lax
from jax.experimental import pallas as pl
from jax.experimental.pallas import tpu as pltpu
from jax.sharding import PartitionSpec as P

RW = 8
MOST = 32
WINDOW = MOST + 2
LAMBDA_REG = 1.0
NX, NY, NZ = 4, 4, 8
MESH = pl.DeviceIdType.MESH

PIECES = (
    ("y", 2, 1, 4, 3, 0, 7),
    ("y", 1, 2, 3, 4, 7, 6),
    ("z", 2, 1, 4, 3, 13, 9),
    ("z", 1, 2, 3, 4, 22, 10),
)
GROUP = 16
PANEL = 64


def children(piece, dy, dz):
    first, yp, ym, zp, zm = PIECES[piece][:5]
    out = []
    if (first == "y" and dz == 0) or first == "z":
        if 0 <= dy < yp:
            out.append((dy + 1, dz))
        if 0 >= dy > -ym:
            out.append((dy - 1, dz))
    if (first == "z" and dy == 0) or first == "y":
        if 0 <= dz < zp:
            out.append((dy, dz + 1))
        if 0 >= dz > -zm:
            out.append((dy, dz - 1))
    return out


def depth(piece, node):
    kids = children(piece, *node)
    return 1 + max(depth(piece, kid) for kid in kids) if kids else 0


def by_depth(piece, node):
    return sorted(children(piece, *node), key=lambda kid: -depth(piece, kid))


def order_of_arrival(late=20.0, lat=1.0, rate=0.082):
    free, heap, count = {}, [], 0

    def send(now, half, piece, par, kid):
        link = (kid[0] - par[0], kid[1] - par[1])
        free[link] = max(now, free.get(link, 0.0)) + PIECES[piece][6] * rate
        heapq.heappush(heap, (free[link] + lat, count, (half, piece, kid)))

    own = [(piece, kid) for piece in range(len(PIECES)) for kid in children(piece, 0, 0)]
    own.sort(key=lambda edge: -depth(*edge))
    for piece, kid in own:
        send(0.0, 0, piece, (0, 0), kid)
        count += 1
    heapq.heappush(heap, (late, count, None))
    count += 1
    order = []
    while heap:
        now, _, what = heapq.heappop(heap)
        order.append(what)
        if what is None:
            todo = [(1, piece, (0, 0), kid) for piece, kid in own]
        else:
            half, piece, node = what
            todo = [(half, piece, node, kid) for kid in by_depth(piece, node)]
        for one in todo:
            send(now, *one)
            count += 1
    return own, order


class RowSum:
    def __init__(self, rows, pair, ring, send_sem, recv_sem, base, my_x, my_core, beside):
        self.rows, self.pair, self.ring = rows, pair, ring
        self.send_sem, self.recv_sem, self.base = send_sem, recv_sem, base
        self.my_x, self.my_core, self.beside = my_x, my_core, beside
        self.half = rows.shape[1] // 2
        self.sent = []

    def chip(self, ahead):
        return (self.my_x + ahead + NX) % NX

    def row(self, ahead, other):
        return self.chip(ahead) * 2 + (1 - self.my_core if other else self.my_core)

    def near(self, ahead, q):
        return pltpu.make_async_remote_copy(
            src_ref=self.rows.at[self.row(ahead, True)],
            dst_ref=self.pair.at[self.chip(ahead)],
            send_sem=self.send_sem.at[self.base + q],
            recv_sem=self.recv_sem.at[self.base + q],
            device_id=self.beside(0, 1),
            device_id_type=MESH,
        )

    def hop(self, slot, ahead, upper, step):
        at = self.base + 4 + slot
        return pltpu.make_async_remote_copy(
            src_ref=self.rows.at[self.row(ahead, False), pl.ds(self.half if upper else 0, self.half)],
            dst_ref=self.ring.at[slot],
            send_sem=self.send_sem.at[at],
            recv_sem=self.recv_sem.at[at],
            device_id=self.beside(step, 0),
            device_id_type=MESH,
        )

    def start(self, *what):
        self.sent.append(self.hop(*what))
        self.sent[-1].start()

    def arrived(self, slot):
        self.hop(slot, 1, False, 1).wait_recv()

    def fold(self, q):
        ahead = (2 - q + NX) % NX
        self.near(ahead, q).wait_recv()
        mine = self.row(ahead, False)
        self.rows[mine] = self.rows[mine] + self.pair[self.chip(ahead)]
        if ahead == 2:
            self.start(0, 2, False, 1)
            self.start(1, 2, True, -1)
        elif ahead == 1:
            self.start(2, 1, True, 1)
        elif ahead == 3:
            self.start(3, 3, False, -1)

    def forward(self):
        half = self.half
        self.arrived(0)
        up = self.row(1, False)
        self.rows[up, 0:half] = self.rows[up, 0:half] + self.ring[0]
        self.start(4, 1, False, 1)
        self.arrived(1)
        back = self.row(3, False)
        self.rows[back, half:2 * half] = self.rows[back, half:2 * half] + self.ring[1]
        self.start(5, 3, True, -1)

    def total(self):
        for slot in (2, 3, 4, 5):
            self.arrived(slot)
        mine, half = self.row(0, False), self.half
        low = self.rows[mine, 0:half] + self.ring[4] + self.ring[3]
        high = self.rows[mine, half:2 * half] + self.ring[5] + self.ring[2]
        return low, high

    def finish(self):
        for q in range(NX):
            self.near((2 - q + NX) % NX, q).wait_send()
        for out in self.sent:
            out.wait_send()


def inverse_2x2(a, b, c):
    scale = 1.0 / (a * c - b * b)
    return c * scale, -b * scale, a * scale


def inverse_4x4(m):
    a, b, c = inverse_2x2(m[0][0], m[0][1], m[1][1])
    top = [[a * m[0][k] + b * m[1][k] for k in (2, 3)], [b * m[0][k] + c * m[1][k] for k in (2, 3)]]

    def rest(k, l):
        return m[k][l] - (m[0][k] * top[0][l - 2] + m[1][k] * top[1][l - 2])

    p, q, r = inverse_2x2(rest(2, 2), rest(2, 3), rest(3, 3))
    side = [[-(top[k][0] * p + top[k][1] * q), -(top[k][0] * q + top[k][1] * r)] for k in (0, 1)]
    aa = a - (side[0][0] * top[0][0] + side[0][1] * top[0][1])
    bb = b - (side[0][0] * top[1][0] + side[0][1] * top[1][1])
    cc = c - (side[1][0] * top[1][0] + side[1][1] * top[1][1])
    return [
        [aa, bb, side[0][0], side[0][1]],
        [bb, cc, side[1][0], side[1][1]],
        [side[0][0], side[1][0], p, q],
        [side[0][1], side[1][1], q, r],
    ]


def small_inverse(block):
    size = block.shape[0]
    down = lax.broadcasted_iota(jnp.int32, (size, size), 0)
    across = lax.broadcasted_iota(jnp.int32, (size, size), 1)
    lane = across[0:8]
    for j in range(0, size, 4):
        cols = [jnp.broadcast_to(block[:, j + k:j + k + 1], (size, size)) for k in range(4)]
        rows = [jnp.broadcast_to(block[j + k:j + k + 1], (8, size)) for k in range(4)]
        pivot = [[jnp.broadcast_to(cols[max(k, l)][j + min(k, l):j + min(k, l) + 1], (8, size)) for l in range(4)] for k in range(4)]
        inverse = inverse_4x4(pivot)
        rest = jnp.where((across >= j) & (across < j + 4), 0.0, block)
        done = []
        for k in range(4):
            row = (inverse[k][0] * rows[0] + inverse[k][1] * rows[1]) + (inverse[k][2] * rows[2] + inverse[k][3] * rows[3])
            for l in range(4):
                row = jnp.where(lane == j + l, inverse[k][l], row)
            done.append(jnp.concatenate([row] * (size // 8), axis=0))
        rest = rest - ((cols[0] * done[0] + cols[1] * done[1]) + (cols[2] * done[2] + cols[3] * done[3]))
        for k in range(4):
            rest = jnp.where(down == j + k, done[k], rest)
        block = rest
    return block


def exact_dot(x, y):
    return jnp.dot(x, y, precision=lax.Precision.HIGHEST, preferred_element_type=jnp.float32)


def eliminate(inv, low, high):
    pivot = small_inverse(inv[low:high, low:high])
    inv[low:high, :] = exact_dot(pivot, inv[low:high, :])
    inv[low:high, low:high] = pivot
    rows = inv[low:high, :]
    for part in ((0, low), (high, inv.shape[0])):
        if part[0] < part[1]:
            cols = inv[part[0]:part[1], low:high]
            inv[part[0]:part[1], low:high] = jnp.zeros_like(cols)
            inv[part[0]:part[1], :] = inv[part[0]:part[1], :] - exact_dot(cols, rows)


def kernel(
    obs_hbm, firsts, rows_s, cols_s, fac_hbm, out_ref, fall0, fall1, obs_v, sel0, sel1, turn0, turn1, masked, eye,
    gram0, gram0_near, gram0_ring, gram1, gram1_near, gram1_ring, rhs0, rhs0_near, rhs0_ring, rhs1, rhs1_near, rhs1_ring,
    rhs_all, inv, whole_gram, send_sem, recv_sem, loc_sem, sum_send, sum_recv
):
    wide = lax.axis_index("wide")
    narrow = lax.axis_index("narrow")
    my_y, my_z = wide // NZ, wide % NZ
    my_x, my_core = narrow // 2, narrow % 2
    own, order = order_of_arrival()
    number = {what: at for at, what in enumerate(order)}
    shard = fac_hbm.shape[0]
    slots = cols_s.shape[0]
    rank = fac_hbm.shape[2]
    half = rank // 2
    lanes, width = obs_v.shape[1:]
    part = lanes // 2
    groups = part // GROUP
    falls, sels, turns = (fall0, fall1), (sel0, sel1), (turn0, turn1)

    def device(dy, dz):
        return (((my_y + dy + NY) % NY) * NZ + (my_z + dz + NZ) % NZ, narrow)

    def beside(dx, other):
        core = 1 - my_core if other else my_core
        return (wide, (my_x + dx + NX) % NX * 2 + core)

    fac_copies = [
        pltpu.make_async_copy(
            fac_hbm.at[:, :, h * half:(h + 1) * half], falls[h].at[pl.ds(wide * shard, shard)], loc_sem.at[h]
        )
        for h in range(2)
    ]
    for one in fac_copies:
        one.start()
    obs_copy = pltpu.make_async_copy(obs_hbm, obs_v, loc_sem.at[2])
    obs_copy.start()

    barrier = pltpu.get_barrier_semaphore()
    partners = [device(*step) for step in ((1, 0), (-1, 0), (0, 1), (0, -1))]
    partners += [beside(0, 1), beside(1, 0), beside(-1, 0)]
    for partner in partners:
        pl.semaphore_signal(barrier, inc=1, device_id=partner, device_id_type=MESH)
    for one in fac_copies:
        one.wait()
    pl.semaphore_wait(barrier, len(partners))

    def copy(h, piece, node, to, step):
        at = number[(h, piece, to)]
        source = ((my_y - node[0] + NY) % NY) * NZ + (my_z - node[1] + NZ) % NZ
        place = falls[h].at[pl.ds(source * shard + PIECES[piece][5], PIECES[piece][6])]
        return pltpu.make_async_remote_copy(
            src_ref=place,
            dst_ref=place,
            send_sem=send_sem.at[at],
            recv_sem=recv_sem.at[at],
            device_id=device(*step),
            device_id_type=MESH,
        )

    sent = []

    def pass_on(h, piece, node, kid):
        sent.append(copy(h, piece, node, kid, (kid[0] - node[0], kid[1] - node[1])))
        sent[-1].start()

    for piece, kid in own:
        pass_on(0, piece, (0, 0), kid)

    down = lax.broadcasted_iota(jnp.int32, (rank, rank), 0)
    across = lax.broadcasted_iota(jnp.int32, (rank, rank), 1)
    lane = lax.broadcasted_iota(jnp.int32, (1, lanes), 1)
    eye[...] = jnp.where(down == across, 1.0, 0.0)[:half, :half].astype(jnp.bfloat16)
    obs_copy.wait()

    gram_sums = [
        RowSum(gram0, gram0_near, gram0_ring, sum_send, sum_recv, 0, my_x, my_core, beside),
        RowSum(gram1, gram1_near, gram1_ring, sum_send, sum_recv, 10, my_x, my_core, beside),
    ]
    rhs_sums = [
        RowSum(rhs0, rhs0_near, rhs0_ring, sum_send, sum_recv, 20, my_x, my_core, beside),
        RowSum(rhs1, rhs1_near, rhs1_ring, sum_send, sum_recv, 30, my_x, my_core, beside),
    ]

    def select(h, step):
        for t in range(2):
            pair = step * 2 + t
            tile = jnp.concatenate(
                [falls[h][cols_s[pair * 2 + k] * groups + g] for k in range(2) for g in range(groups)], axis=0
            )
            sels[h][pair] = tile
            flat = lax.dot_general(eye[...], tile, (((1,), (1,)), ((), ())), preferred_element_type=jnp.float32)
            turns[h][pair] = flat.astype(jnp.bfloat16)

    pairs = WINDOW // 2

    def mask(h, row):
        first = firsts[row]
        for t in range(pairs):
            keep = [jnp.where(rows_s[(first + t) * 2 + k] == row, 1.0, 0.0) for k in range(2)]
            keep = jnp.where(lane < part, keep[0], keep[1]).astype(jnp.bfloat16)
            masked[:, t * lanes:(t + 1) * lanes] = turns[h][first + t] * keep

    def product(first, load):
        total = None
        for t in range(0, pairs, 2):
            both = [load(first + k) for k in range(t, min(t + 2, pairs))]
            left = masked[:, t * lanes:(t + len(both)) * lanes]
            right = both[0] if len(both) == 1 else jnp.concatenate(both, axis=0)
            one = jnp.dot(left, right, preferred_element_type=jnp.float32)
            total = one if total is None else total + one
        return total

    def gram_of(h, row):
        if h == 0:
            gram0[row] = product(firsts[row], lambda at: sel0[at])
        else:
            gram1[row] = product(firsts[row], lambda at: jnp.concatenate([sel0[at], sel1[at]], axis=1))

    def rhs_of(h, row, tile):
        at = slice(tile * rank, (tile + 1) * rank)
        (rhs0, rhs1)[h][row, :, at] = product(firsts[row], lambda pair: obs_v[pair, :, at])

    def row_of(q, other):
        return gram_sums[0].row((2 - q + NX) % NX, other)

    def near(sums, q):
        sums.near((2 - q + NX) % NX, q).start()

    wide_tiles = width // rank
    steps = slots // 4
    jobs = []
    for step in range(0, steps, 2):
        jobs.append(lambda step=step: (select(0, step), select(0, step + 1)))
    for q in range(NX):
        for other in (True, False):
            jobs.append(lambda q=q, other=other: (mask(0, row_of(q, other)), gram_of(0, row_of(q, other))))
            if other:
                jobs[-1] = lambda q=q: (mask(0, row_of(q, True)), gram_of(0, row_of(q, True)), near(gram_sums[0], q))
            for tile in range(wide_tiles):
                jobs.append(lambda q=q, other=other, tile=tile: rhs_of(0, row_of(q, other), tile))
        jobs.append(lambda q=q: rhs_sums[0].near((2 - q + NX) % NX, q).start())
    for q in range(NX):
        jobs.append(lambda q=q: gram_sums[0].fold(q))
    for q in range(NX):
        jobs.append(lambda q=q: rhs_sums[0].fold(q))
    jobs.append(gram_sums[0].forward)
    jobs.append(rhs_sums[0].forward)

    ready = max(at for at, what in enumerate(order) if what is not None and what[0] == 0)
    done = 0
    for at, what in enumerate(order):
        if what is None:
            for piece, kid in own:
                pass_on(1, piece, (0, 0), kid)
            continue
        h, piece, node = what
        copy(h, piece, node, node, (1, 0)).wait_recv()
        for kid in by_depth(piece, node):
            pass_on(h, piece, node, kid)
        while done < len(jobs) and at >= ready and done * (len(order) - 1 - ready) <= (at - ready) * len(jobs):
            jobs[done]()
            done += 1
    while done < len(jobs):
        jobs[done]()
        done += 1

    pl.loop(0, steps)(functools.partial(select, 1))

    @pl.loop(0, NX)
    def grams(q):
        for other in (True, False):
            mask(1, row_of(q, other))
            gram_of(1, row_of(q, other))
            if other:
                near(gram_sums[1], q)

    def rhs_pair(q):
        for other in (True, False):
            mask(1, row_of(q, other))
            for tile in range(wide_tiles):
                rhs_of(1, row_of(q, other), tile)
            if other:
                near(rhs_sums[1], q)

    for q in range(NX):
        gram_sums[1].fold(q)
    pl.loop(0, 2)(rhs_pair)
    gram_sums[1].forward()
    rhs_sums[1].fold(0)
    rhs_sums[1].fold(1)
    pl.loop(2, NX)(rhs_pair)
    rhs_sums[1].fold(2)
    rhs_sums[1].fold(3)

    rhs_all[:, :half] = jnp.concatenate(rhs_sums[0].total(), axis=0).T
    same = jnp.where(down == across, LAMBDA_REG, 0.0)
    upper = jnp.concatenate(gram_sums[0].total(), axis=0)
    lower = jnp.concatenate(gram_sums[1].total(), axis=0)
    inv[:half, :half] = upper + same[:half, :half]
    inv[half:, :] = lower + same[half:, :]
    inv[:half, half:] = lower[:, :half].T
    whole_gram[...] = inv[...]
    for p in range(rank // PANEL):
        if p == 1:
            rhs_sums[1].forward()
        eliminate(inv, p * PANEL, (p + 1) * PANEL)

    rhs_all[:, half:] = jnp.concatenate(rhs_sums[1].total(), axis=0).T
    for tile in range(wide_tiles):
        at = slice(tile * rank, (tile + 1) * rank)
        total = rhs_all[at]
        first = exact_dot(total, inv[...])
        out_ref[at] = first + exact_dot(total - exact_dot(first, whole_gram[...]), inv[...])

    for sums in gram_sums + rhs_sums:
        sums.finish()
    for out in sent:
        out.wait_send()


def solved_row(obs, rows, cols, factors):
    slots, part, width = obs.shape
    rank = factors.shape[-1]
    half = rank // 2
    edges = len(order_of_arrival()[1])
    every = NY * NZ * RW * part // GROUP

    def sums(rows, cols):
        return [
            pltpu.VMEM((RW, rows, cols), jnp.float32),
            pltpu.VMEM((NX, rows, cols), jnp.float32),
            pltpu.VMEM((6, rows // 2, cols), jnp.float32),
        ]

    return pl.pallas_call(
        kernel,
        out_shape=jax.ShapeDtypeStruct((width, rank), jnp.float32),
        in_specs=[
            pl.BlockSpec(memory_space=pl.ANY),
            pl.BlockSpec(memory_space=pltpu.SMEM),
            pl.BlockSpec(memory_space=pltpu.SMEM),
            pl.BlockSpec(memory_space=pltpu.SMEM),
            pl.BlockSpec(memory_space=pl.ANY),
        ],
        out_specs=pl.BlockSpec(memory_space=pltpu.VMEM),
        scratch_shapes=[
            pltpu.VMEM((every, GROUP, half), jnp.bfloat16),
            pltpu.VMEM((every, GROUP, half), jnp.bfloat16),
            pltpu.VMEM((slots // 2, 2 * part, width), jnp.bfloat16),
            pltpu.VMEM((slots // 2, 2 * part, half), jnp.bfloat16),
            pltpu.VMEM((slots // 2, 2 * part, half), jnp.bfloat16),
            pltpu.VMEM((slots // 2, half, 2 * part), jnp.bfloat16),
            pltpu.VMEM((slots // 2, half, 2 * part), jnp.bfloat16),
            pltpu.VMEM((half, WINDOW * part), jnp.bfloat16),
            pltpu.VMEM((half, half), jnp.bfloat16),
            *sums(half, half),
            *sums(half, rank),
            *sums(half, width),
            *sums(half, width),
            pltpu.VMEM((width, rank), jnp.float32),
            pltpu.VMEM((rank, rank), jnp.float32),
            pltpu.VMEM((rank, rank), jnp.float32),
            pltpu.SemaphoreType.DMA((edges,)),
            pltpu.SemaphoreType.DMA((edges,)),
            pltpu.SemaphoreType.DMA((3,)),
            pltpu.SemaphoreType.DMA((40,)),
            pltpu.SemaphoreType.DMA((40,)),
        ],
        compiler_params=pltpu.CompilerParams(collective_id=0, has_side_effects=True, vmem_limit_bytes=60 * 1024 * 1024),
        name="solve_rows",
    )(
        obs.reshape(slots // 2, 2 * part, width),
        window_starts(rows),
        rows,
        cols,
        factors.reshape(-1, GROUP, rank),
    )


def window_starts(rows):
    before = jnp.sum((rows[None, :] < jnp.arange(RW, dtype=jnp.int32)[:, None]).astype(jnp.int32), axis=1)
    return jnp.minimum(before // 2, (rows.shape[0] - WINDOW) // 2)


def body(obs_blocks, obs_row, obs_col, factors):
    return solved_row(obs_blocks[0], obs_row[0], obs_col[0], factors)[None]


def solution(mesh):
    placed = (
        P("wide", None, "narrow", None),
        P("wide", None),
        P("wide", None),
        P("wide", "narrow", None),
    )
    return jax.shard_map(
        body,
        mesh=mesh,
        in_specs=placed,
        out_specs=P(("wide", "narrow"), None, None),
        check_vma=False,
    )
```

```python
import functools
import heapq

import jax
import jax.numpy as jnp
from jax import lax
from jax.experimental import pallas as pl
from jax.experimental.pallas import tpu as pltpu
from jax.sharding import PartitionSpec as P

RW = 8
MOST = 32
WINDOW = MOST + 2
LAMBDA_REG = 1.0
NX, NY, NZ = 4, 4, 8
MESH = pl.DeviceIdType.MESH

PIECES = (
    ("y", 2, 1, 4, 3, 0, 7),
    ("y", 1, 2, 3, 4, 7, 6),
    ("z", 2, 1, 4, 3, 13, 9),
    ("z", 1, 2, 3, 4, 22, 10),
)
GROUP = 16
PANEL = 64
AT_ONCE = 8


def children(piece, dy, dz):
    first, yp, ym, zp, zm = PIECES[piece][:5]
    out = []
    if (first == "y" and dz == 0) or first == "z":
        if 0 <= dy < yp:
            out.append((dy + 1, dz))
        if 0 >= dy > -ym:
            out.append((dy - 1, dz))
    if (first == "z" and dy == 0) or first == "y":
        if 0 <= dz < zp:
            out.append((dy, dz + 1))
        if 0 >= dz > -zm:
            out.append((dy, dz - 1))
    return out


def depth(piece, node):
    kids = children(piece, *node)
    return 1 + max(depth(piece, kid) for kid in kids) if kids else 0


def by_depth(piece, node):
    return sorted(children(piece, *node), key=lambda kid: -depth(piece, kid))


def order_of_arrival(late=20.0, lat=1.0, rate=0.082):
    free, heap, count = {}, [], 0

    def send(now, half, piece, par, kid):
        link = (kid[0] - par[0], kid[1] - par[1])
        free[link] = max(now, free.get(link, 0.0)) + PIECES[piece][6] * rate
        heapq.heappush(heap, (free[link] + lat, count, (half, piece, kid)))

    own = [(piece, kid) for piece in range(len(PIECES)) for kid in children(piece, 0, 0)]
    own.sort(key=lambda edge: -depth(*edge))
    for piece, kid in own:
        send(0.0, 0, piece, (0, 0), kid)
        count += 1
    heapq.heappush(heap, (late, count, None))
    count += 1
    order = []
    while heap:
        now, _, what = heapq.heappop(heap)
        order.append(what)
        if what is None:
            todo = [(1, piece, (0, 0), kid) for piece, kid in own]
        else:
            half, piece, node = what
            todo = [(half, piece, node, kid) for kid in by_depth(piece, node)]
        for one in todo:
            send(now, *one)
            count += 1
    return own, order


class RowSum:
    def __init__(self, rows, pair, ring, send_sem, recv_sem, base, my_x, my_core, beside):
        self.rows, self.pair, self.ring = rows, pair, ring
        self.send_sem, self.recv_sem, self.base = send_sem, recv_sem, base
        self.my_x, self.my_core, self.beside = my_x, my_core, beside
        self.half = rows.shape[1] // 2
        self.sent = []

    def chip(self, ahead):
        return (self.my_x + ahead + NX) % NX

    def row(self, ahead, other):
        return self.chip(ahead) * 2 + (1 - self.my_core if other else self.my_core)

    def near(self, ahead, q):
        return pltpu.make_async_remote_copy(
            src_ref=self.rows.at[self.row(ahead, True)],
            dst_ref=self.pair.at[self.chip(ahead)],
            send_sem=self.send_sem.at[self.base + q],
            recv_sem=self.recv_sem.at[self.base + q],
            device_id=self.beside(0, 1),
            device_id_type=MESH,
        )

    def hop(self, slot, ahead, upper, step):
        at = self.base + 4 + slot
        return pltpu.make_async_remote_copy(
            src_ref=self.rows.at[self.row(ahead, False), pl.ds(self.half if upper else 0, self.half)],
            dst_ref=self.ring.at[slot],
            send_sem=self.send_sem.at[at],
            recv_sem=self.recv_sem.at[at],
            device_id=self.beside(step, 0),
            device_id_type=MESH,
        )

    def start(self, *what):
        self.sent.append(self.hop(*what))
        self.sent[-1].start()

    def arrived(self, slot):
        self.hop(slot, 1, False, 1).wait_recv()

    def fold(self, q):
        ahead = (2 - q + NX) % NX
        self.near(ahead, q).wait_recv()
        mine = self.row(ahead, False)
        self.rows[mine] = self.rows[mine] + self.pair[self.chip(ahead)]
        if ahead == 2:
            self.start(0, 2, False, 1)
            self.start(1, 2, True, -1)
        elif ahead == 1:
            self.start(2, 1, True, 1)
        elif ahead == 3:
            self.start(3, 3, False, -1)

    def forward(self):
        half = self.half
        self.arrived(0)
        up = self.row(1, False)
        self.rows[up, 0:half] = self.rows[up, 0:half] + self.ring[0]
        self.start(4, 1, False, 1)
        self.arrived(1)
        back = self.row(3, False)
        self.rows[back, half:2 * half] = self.rows[back, half:2 * half] + self.ring[1]
        self.start(5, 3, True, -1)

    def total(self):
        for slot in (2, 3, 4, 5):
            self.arrived(slot)
        mine, half = self.row(0, False), self.half
        low = self.rows[mine, 0:half] + self.ring[4] + self.ring[3]
        high = self.rows[mine, half:2 * half] + self.ring[5] + self.ring[2]
        return low, high

    def finish(self):
        for q in range(NX):
            self.near((2 - q + NX) % NX, q).wait_send()
        for out in self.sent:
            out.wait_send()


def inverse_2x2(a, b, c):
    scale = 1.0 / (a * c - b * b)
    return c * scale, -b * scale, a * scale


def inverse_4x4(m):
    a, b, c = inverse_2x2(m[0][0], m[0][1], m[1][1])
    top = [[a * m[0][k] + b * m[1][k] for k in (2, 3)], [b * m[0][k] + c * m[1][k] for k in (2, 3)]]

    def rest(k, l):
        return m[k][l] - (m[0][k] * top[0][l - 2] + m[1][k] * top[1][l - 2])

    p, q, r = inverse_2x2(rest(2, 2), rest(2, 3), rest(3, 3))
    side = [[-(top[k][0] * p + top[k][1] * q), -(top[k][0] * q + top[k][1] * r)] for k in (0, 1)]
    aa = a - (side[0][0] * top[0][0] + side[0][1] * top[0][1])
    bb = b - (side[0][0] * top[1][0] + side[0][1] * top[1][1])
    cc = c - (side[1][0] * top[1][0] + side[1][1] * top[1][1])
    return [
        [aa, bb, side[0][0], side[0][1]],
        [bb, cc, side[1][0], side[1][1]],
        [side[0][0], side[1][0], p, q],
        [side[0][1], side[1][1], q, r],
    ]


def small_inverse(block):
    size = block.shape[0]
    down = lax.broadcasted_iota(jnp.int32, (size, size), 0)
    across = lax.broadcasted_iota(jnp.int32, (size, size), 1)
    lane = across[0:8]

    def spread(values, j):
        return [jnp.broadcast_to(values[:, j + k:j + k + 1], (size, size)) for k in range(4)]

    def tall(row):
        return jnp.concatenate([row] * (size // 8), axis=0)

    def mix(weights, rows):
        return (weights[0] * rows[0] + weights[1] * rows[1]) + (weights[2] * rows[2] + weights[3] * rows[3])

    cols = spread(block, 0)
    for j in range(0, size, 4):
        later = spread(block, j + 4) if j + 4 < size else []
        pivot = [[jnp.broadcast_to(cols[max(k, l)][j + min(k, l):j + min(k, l) + 1], (8, size)) for l in range(4)] for k in range(4)]
        inverse = inverse_4x4(pivot)
        ahead = []
        for old in later:
            here = [jnp.broadcast_to(old[j + k:j + k + 1], (8, size)) for k in range(4)]
            new_rows = [tall(mix(inverse[k], here)) for k in range(4)]
            new = old - mix(cols, new_rows)
            for k in range(4):
                new = jnp.where(down == j + k, new_rows[k], new)
            ahead.append(new)
        rows = [jnp.broadcast_to(block[j + k:j + k + 1], (8, size)) for k in range(4)]
        done = []
        for k in range(4):
            row = mix(inverse[k], rows)
            for l in range(4):
                row = jnp.where(lane == j + l, inverse[k][l], row)
            done.append(tall(row))
        block = jnp.where((across >= j) & (across < j + 4), 0.0, block) - mix(cols, done)
        for k in range(4):
            block = jnp.where(down == j + k, done[k], block)
        cols = ahead
    return block


def exact_dot(x, y):
    return jnp.dot(x, y, precision=lax.Precision.HIGHEST, preferred_element_type=jnp.float32)


def eliminate(inv, low, high):
    pivot = small_inverse(inv[low:high, low:high])
    inv[low:high, :] = exact_dot(pivot, inv[low:high, :])
    inv[low:high, low:high] = pivot
    rows = inv[low:high, :]
    for part in ((0, low), (high, inv.shape[0])):
        if part[0] < part[1]:
            cols = inv[part[0]:part[1], low:high]
            inv[part[0]:part[1], low:high] = jnp.zeros_like(cols)
            inv[part[0]:part[1], :] = inv[part[0]:part[1], :] - exact_dot(cols, rows)


def kernel(
    obs_hbm, firsts, rows_s, cols_s, fac_hbm, out_ref, fall0, fall1, obs_v, sel0, sel1, turn0, turn1, keeps, masked, eye,
    gram0, gram0_near, gram0_ring, gram1, gram1_near, gram1_ring, rhs0, rhs0_near, rhs0_ring, rhs1, rhs1_near, rhs1_ring,
    rhs_all, inv, whole_gram, send_sem, recv_sem, loc_sem, sum_send, sum_recv
):
    wide = lax.axis_index("wide")
    narrow = lax.axis_index("narrow")
    my_y, my_z = wide // NZ, wide % NZ
    my_x, my_core = narrow // 2, narrow % 2
    own, order = order_of_arrival()
    number = {what: at for at, what in enumerate(order)}
    shard = fac_hbm.shape[0]
    slots = cols_s.shape[0]
    rank = fac_hbm.shape[2]
    half = rank // 2
    lanes, width = obs_v.shape[1:]
    part = lanes // 2
    groups = part // GROUP
    falls, sels, turns = (fall0, fall1), (sel0, sel1), (turn0, turn1)

    def device(dy, dz):
        return (((my_y + dy + NY) % NY) * NZ + (my_z + dz + NZ) % NZ, narrow)

    def beside(dx, other):
        core = 1 - my_core if other else my_core
        return (wide, (my_x + dx + NX) % NX * 2 + core)

    fac_copies = [
        pltpu.make_async_copy(
            fac_hbm.at[:, :, h * half:(h + 1) * half], falls[h].at[pl.ds(wide * shard, shard)], loc_sem.at[h]
        )
        for h in range(2)
    ]
    for one in fac_copies:
        one.start()
    obs_copy = pltpu.make_async_copy(obs_hbm, obs_v, loc_sem.at[2])
    obs_copy.start()

    barrier = pltpu.get_barrier_semaphore()
    partners = [device(*step) for step in ((1, 0), (-1, 0), (0, 1), (0, -1))]
    partners += [beside(0, 1), beside(1, 0), beside(-1, 0)]
    for partner in partners:
        pl.semaphore_signal(barrier, inc=1, device_id=partner, device_id_type=MESH)
    for one in fac_copies:
        one.wait()
    pl.semaphore_wait(barrier, len(partners))

    def copy(h, piece, node, to, step):
        at = number[(h, piece, to)]
        source = ((my_y - node[0] + NY) % NY) * NZ + (my_z - node[1] + NZ) % NZ
        place = falls[h].at[pl.ds(source * shard + PIECES[piece][5], PIECES[piece][6])]
        return pltpu.make_async_remote_copy(
            src_ref=place,
            dst_ref=place,
            send_sem=send_sem.at[at],
            recv_sem=recv_sem.at[at],
            device_id=device(*step),
            device_id_type=MESH,
        )

    sent = []

    def pass_on(h, piece, node, kid):
        sent.append(copy(h, piece, node, kid, (kid[0] - node[0], kid[1] - node[1])))
        sent[-1].start()

    for piece, kid in own:
        pass_on(0, piece, (0, 0), kid)

    down = lax.broadcasted_iota(jnp.int32, (rank, rank), 0)
    across = lax.broadcasted_iota(jnp.int32, (rank, rank), 1)
    lane = lax.broadcasted_iota(jnp.int32, (GROUP, lanes), 1)
    eye[...] = jnp.where(down == across, 1.0, 0.0)[:half, :half].astype(jnp.bfloat16)
    obs_copy.wait()

    gram_sums = [
        RowSum(gram0, gram0_near, gram0_ring, sum_send, sum_recv, 0, my_x, my_core, beside),
        RowSum(gram1, gram1_near, gram1_ring, sum_send, sum_recv, 10, my_x, my_core, beside),
    ]
    rhs_sums = [
        RowSum(rhs0, rhs0_near, rhs0_ring, sum_send, sum_recv, 20, my_x, my_core, beside),
        RowSum(rhs1, rhs1_near, rhs1_ring, sum_send, sum_recv, 30, my_x, my_core, beside),
    ]

    def select(h, step):
        for t in range(AT_ONCE):
            pair = step * AT_ONCE + t
            tile = jnp.concatenate(
                [falls[h][cols_s[pair * 2 + k] * groups + g] for k in range(2) for g in range(groups)], axis=0
            )
            sels[h][pair] = tile
            flat = lax.dot_general(eye[...], tile, (((1,), (1,)), ((), ())), preferred_element_type=jnp.float32)
            turns[h][pair] = flat.astype(jnp.bfloat16)

    pairs = WINDOW // 2

    def keep_of(row):
        first = firsts[row]
        for t in range(pairs):
            keep = [jnp.where(rows_s[(first + t) * 2 + k] == row, 1.0, 0.0) for k in range(2)]
            keeps[row, t] = jnp.where(lane < part, keep[0], keep[1]).astype(jnp.bfloat16)

    def mask(h, row):
        first = firsts[row]
        for t in range(pairs):
            keep = jnp.concatenate([keeps[row, t]] * (half // GROUP), axis=0)
            masked[row, :, t * lanes:(t + 1) * lanes] = turns[h][first + t] * keep

    def product(row, load):
        first, total = firsts[row], None
        for t in range(0, pairs, 2):
            both = [load(first + k) for k in range(t, min(t + 2, pairs))]
            left = masked[row, :, t * lanes:(t + len(both)) * lanes]
            right = both[0] if len(both) == 1 else jnp.concatenate(both, axis=0)
            one = jnp.dot(left, right, preferred_element_type=jnp.float32)
            total = one if total is None else total + one
        return total

    def gram_of(h, row):
        if h == 0:
            gram0[row] = product(row, lambda at: sel0[at])
        else:
            gram1[row] = product(row, lambda at: jnp.concatenate([sel0[at], sel1[at]], axis=1))

    def rhs_of(h, row, tile):
        at = slice(tile * rank, (tile + 1) * rank)
        (rhs0, rhs1)[h][row, :, at] = product(row, lambda pair: obs_v[pair, :, at])

    def row_of(q, other):
        return gram_sums[0].row((2 - q + NX) % NX, other)

    def near(sums, q):
        sums.near((2 - q + NX) % NX, q).start()

    wide_tiles = width // rank
    steps = slots // 2 // AT_ONCE
    jobs = []
    for step in range(steps):
        jobs.append(lambda step=step: select(0, step))
    for q in range(NX):
        for other in (True, False):
            jobs.append(lambda q=q, other=other: (mask(0, row_of(q, other)), gram_of(0, row_of(q, other))))
            if other:
                jobs[-1] = lambda q=q: (mask(0, row_of(q, True)), gram_of(0, row_of(q, True)), near(gram_sums[0], q))
            for tile in range(wide_tiles):
                jobs.append(lambda q=q, other=other, tile=tile: rhs_of(0, row_of(q, other), tile))
        jobs.append(lambda q=q: rhs_sums[0].near((2 - q + NX) % NX, q).start())
    for q in range(NX):
        jobs.append(lambda q=q: gram_sums[0].fold(q))
    for q in range(NX):
        jobs.append(lambda q=q: rhs_sums[0].fold(q))
    jobs.append(gram_sums[0].forward)
    jobs.append(rhs_sums[0].forward)

    pl.loop(0, RW)(keep_of)
    ready = max(at for at, what in enumerate(order) if what is not None and what[0] == 0)
    done = 0
    for at, what in enumerate(order):
        if what is None:
            for piece, kid in own:
                pass_on(1, piece, (0, 0), kid)
            continue
        h, piece, node = what
        copy(h, piece, node, node, (1, 0)).wait_recv()
        for kid in by_depth(piece, node):
            pass_on(h, piece, node, kid)
        while done < len(jobs) and at >= ready and done * (len(order) - 1 - ready) <= (at - ready) * len(jobs):
            jobs[done]()
            done += 1
    while done < len(jobs):
        jobs[done]()
        done += 1

    pl.loop(0, steps)(functools.partial(select, 1))

    @pl.loop(0, NX)
    def grams(q):
        for other in (True, False):
            mask(1, row_of(q, other))
            gram_of(1, row_of(q, other))
            if other:
                near(gram_sums[1], q)

    def rhs_pair(q):
        for other in (True, False):
            for tile in range(wide_tiles):
                rhs_of(1, row_of(q, other), tile)
            if other:
                near(rhs_sums[1], q)

    for q in range(NX):
        gram_sums[1].fold(q)
    pl.loop(0, 2)(rhs_pair)
    gram_sums[1].forward()
    rhs_sums[1].fold(0)
    rhs_sums[1].fold(1)
    pl.loop(2, NX)(rhs_pair)
    rhs_sums[1].fold(2)
    rhs_sums[1].fold(3)

    rhs_all[:, :half] = jnp.concatenate(rhs_sums[0].total(), axis=0).T
    same = jnp.where(down == across, LAMBDA_REG, 0.0)
    upper = jnp.concatenate(gram_sums[0].total(), axis=0)
    lower = jnp.concatenate(gram_sums[1].total(), axis=0)
    inv[:half, :half] = upper + same[:half, :half]
    inv[half:, :] = lower + same[half:, :]
    inv[:half, half:] = lower[:, :half].T
    whole_gram[...] = inv[...]
    for p in range(rank // PANEL):
        if p == 1:
            rhs_sums[1].forward()
        eliminate(inv, p * PANEL, (p + 1) * PANEL)

    rhs_all[:, half:] = jnp.concatenate(rhs_sums[1].total(), axis=0).T
    for tile in range(wide_tiles):
        at = slice(tile * rank, (tile + 1) * rank)
        total = rhs_all[at]
        first = exact_dot(total, inv[...])
        out_ref[at] = first + exact_dot(total - exact_dot(first, whole_gram[...]), inv[...])

    for sums in gram_sums + rhs_sums:
        sums.finish()
    for out in sent:
        out.wait_send()


def solved_row(obs, rows, cols, factors):
    slots, part, width = obs.shape
    rank = factors.shape[-1]
    half = rank // 2
    edges = len(order_of_arrival()[1])
    every = NY * NZ * RW * part // GROUP

    def sums(rows, cols):
        return [
            pltpu.VMEM((RW, rows, cols), jnp.float32),
            pltpu.VMEM((NX, rows, cols), jnp.float32),
            pltpu.VMEM((6, rows // 2, cols), jnp.float32),
        ]

    return pl.pallas_call(
        kernel,
        out_shape=jax.ShapeDtypeStruct((width, rank), jnp.float32),
        in_specs=[
            pl.BlockSpec(memory_space=pl.ANY),
            pl.BlockSpec(memory_space=pltpu.SMEM),
            pl.BlockSpec(memory_space=pltpu.SMEM),
            pl.BlockSpec(memory_space=pltpu.SMEM),
            pl.BlockSpec(memory_space=pl.ANY),
        ],
        out_specs=pl.BlockSpec(memory_space=pltpu.VMEM),
        scratch_shapes=[
            pltpu.VMEM((every, GROUP, half), jnp.bfloat16),
            pltpu.VMEM((every, GROUP, half), jnp.bfloat16),
            pltpu.VMEM((slots // 2, 2 * part, width), jnp.bfloat16),
            pltpu.VMEM((slots // 2, 2 * part, half), jnp.bfloat16),
            pltpu.VMEM((slots // 2, 2 * part, half), jnp.bfloat16),
            pltpu.VMEM((slots // 2, half, 2 * part), jnp.bfloat16),
            pltpu.VMEM((slots // 2, half, 2 * part), jnp.bfloat16),
            pltpu.VMEM((RW, WINDOW // 2, GROUP, 2 * part), jnp.bfloat16),
            pltpu.VMEM((RW, half, WINDOW * part), jnp.bfloat16),
            pltpu.VMEM((half, half), jnp.bfloat16),
            *sums(half, half),
            *sums(half, rank),
            *sums(half, width),
            *sums(half, width),
            pltpu.VMEM((width, rank), jnp.float32),
            pltpu.VMEM((rank, rank), jnp.float32),
            pltpu.VMEM((rank, rank), jnp.float32),
            pltpu.SemaphoreType.DMA((edges,)),
            pltpu.SemaphoreType.DMA((edges,)),
            pltpu.SemaphoreType.DMA((3,)),
            pltpu.SemaphoreType.DMA((40,)),
            pltpu.SemaphoreType.DMA((40,)),
        ],
        compiler_params=pltpu.CompilerParams(collective_id=0, has_side_effects=True, vmem_limit_bytes=60 * 1024 * 1024),
        name="solve_rows",
    )(
        obs.reshape(slots // 2, 2 * part, width),
        window_starts(rows),
        rows,
        cols,
        factors.reshape(-1, GROUP, rank),
    )


def window_starts(rows):
    before = jnp.sum((rows[None, :] < jnp.arange(RW, dtype=jnp.int32)[:, None]).astype(jnp.int32), axis=1)
    return jnp.minimum(before // 2, (rows.shape[0] - WINDOW) // 2)


def body(obs_blocks, obs_row, obs_col, factors):
    return solved_row(obs_blocks[0], obs_row[0], obs_col[0], factors)[None]


def solution(mesh):
    placed = (
        P("wide", None, "narrow", None),
        P("wide", None),
        P("wide", None),
        P("wide", "narrow", None),
    )
    return jax.shard_map(
        body,
        mesh=mesh,
        in_specs=placed,
        out_specs=P(("wide", "narrow"), None, None),
        check_vma=False,
    )
```

```python
import functools
import heapq

import jax
import jax.numpy as jnp
from jax import lax
from jax.experimental import pallas as pl
from jax.experimental.pallas import tpu as pltpu
from jax.sharding import PartitionSpec as P

RW = 8
MOST = 32
WINDOW = MOST + 2
LAMBDA_REG = 1.0
NX, NY, NZ = 4, 4, 8
MESH = pl.DeviceIdType.MESH

PIECES = (
    ("y", 2, 1, 4, 3, 0, 7),
    ("y", 1, 2, 3, 4, 7, 6),
    ("z", 2, 1, 4, 3, 13, 9),
    ("z", 1, 2, 3, 4, 22, 10),
)
GROUP = 16
PANEL = 64
AT_ONCE = 8


def children(piece, dy, dz):
    first, yp, ym, zp, zm = PIECES[piece][:5]
    out = []
    if (first == "y" and dz == 0) or first == "z":
        if 0 <= dy < yp:
            out.append((dy + 1, dz))
        if 0 >= dy > -ym:
            out.append((dy - 1, dz))
    if (first == "z" and dy == 0) or first == "y":
        if 0 <= dz < zp:
            out.append((dy, dz + 1))
        if 0 >= dz > -zm:
            out.append((dy, dz - 1))
    return out


def depth(piece, node):
    kids = children(piece, *node)
    return 1 + max(depth(piece, kid) for kid in kids) if kids else 0


def by_depth(piece, node):
    return sorted(children(piece, *node), key=lambda kid: -depth(piece, kid))


def order_of_arrival(late=20.0, lat=1.0, rate=0.082):
    free, heap, count = {}, [], 0

    def send(now, half, piece, par, kid):
        link = (kid[0] - par[0], kid[1] - par[1])
        free[link] = max(now, free.get(link, 0.0)) + PIECES[piece][6] * rate
        heapq.heappush(heap, (free[link] + lat, count, (half, piece, kid)))

    own = [(piece, kid) for piece in range(len(PIECES)) for kid in children(piece, 0, 0)]
    own.sort(key=lambda edge: -depth(*edge))
    for piece, kid in own:
        send(0.0, 0, piece, (0, 0), kid)
        count += 1
    heapq.heappush(heap, (late, count, None))
    count += 1
    order = []
    while heap:
        now, _, what = heapq.heappop(heap)
        order.append(what)
        if what is None:
            todo = [(1, piece, (0, 0), kid) for piece, kid in own]
        else:
            half, piece, node = what
            todo = [(half, piece, node, kid) for kid in by_depth(piece, node)]
        for one in todo:
            send(now, *one)
            count += 1
    return own, order


class RowSum:
    def __init__(self, rows, pair, ring, send_sem, recv_sem, base, my_x, my_core, beside):
        self.rows, self.pair, self.ring = rows, pair, ring
        self.send_sem, self.recv_sem, self.base = send_sem, recv_sem, base
        self.my_x, self.my_core, self.beside = my_x, my_core, beside
        self.half = rows.shape[1] // 2
        self.sent = []

    def chip(self, ahead):
        return (self.my_x + ahead + NX) % NX

    def row(self, ahead, other):
        return self.chip(ahead) * 2 + (1 - self.my_core if other else self.my_core)

    def near(self, ahead, q):
        return pltpu.make_async_remote_copy(
            src_ref=self.rows.at[self.row(ahead, True)],
            dst_ref=self.pair.at[self.chip(ahead)],
            send_sem=self.send_sem.at[self.base + q],
            recv_sem=self.recv_sem.at[self.base + q],
            device_id=self.beside(0, 1),
            device_id_type=MESH,
        )

    def hop(self, slot, ahead, upper, step):
        at = self.base + 4 + slot
        return pltpu.make_async_remote_copy(
            src_ref=self.rows.at[self.row(ahead, False), pl.ds(self.half if upper else 0, self.half)],
            dst_ref=self.ring.at[slot],
            send_sem=self.send_sem.at[at],
            recv_sem=self.recv_sem.at[at],
            device_id=self.beside(step, 0),
            device_id_type=MESH,
        )

    def start(self, *what):
        self.sent.append(self.hop(*what))
        self.sent[-1].start()

    def arrived(self, slot):
        self.hop(slot, 1, False, 1).wait_recv()

    def fold(self, q):
        ahead = (2 - q + NX) % NX
        self.near(ahead, q).wait_recv()
        mine = self.row(ahead, False)
        self.rows[mine] = self.rows[mine] + self.pair[self.chip(ahead)]
        if ahead == 2:
            self.start(0, 2, False, 1)
            self.start(1, 2, True, -1)
        elif ahead == 1:
            self.start(2, 1, True, 1)
        elif ahead == 3:
            self.start(3, 3, False, -1)

    def forward(self):
        half = self.half
        self.arrived(0)
        up = self.row(1, False)
        self.rows[up, 0:half] = self.rows[up, 0:half] + self.ring[0]
        self.start(4, 1, False, 1)
        self.arrived(1)
        back = self.row(3, False)
        self.rows[back, half:2 * half] = self.rows[back, half:2 * half] + self.ring[1]
        self.start(5, 3, True, -1)

    def total(self):
        for slot in (2, 3, 4, 5):
            self.arrived(slot)
        mine, half = self.row(0, False), self.half
        low = self.rows[mine, 0:half] + self.ring[4] + self.ring[3]
        high = self.rows[mine, half:2 * half] + self.ring[5] + self.ring[2]
        return low, high

    def finish(self):
        for q in range(NX):
            self.near((2 - q + NX) % NX, q).wait_send()
        for out in self.sent:
            out.wait_send()


def inverse_2x2(a, b, c):
    scale = 1.0 / (a * c - b * b)
    return c * scale, -b * scale, a * scale


def inverse_4x4(m):
    a, b, c = inverse_2x2(m[0][0], m[0][1], m[1][1])
    top = [[a * m[0][k] + b * m[1][k] for k in (2, 3)], [b * m[0][k] + c * m[1][k] for k in (2, 3)]]

    def rest(k, l):
        return m[k][l] - (m[0][k] * top[0][l - 2] + m[1][k] * top[1][l - 2])

    p, q, r = inverse_2x2(rest(2, 2), rest(2, 3), rest(3, 3))
    side = [[-(top[k][0] * p + top[k][1] * q), -(top[k][0] * q + top[k][1] * r)] for k in (0, 1)]
    aa = a - (side[0][0] * top[0][0] + side[0][1] * top[0][1])
    bb = b - (side[0][0] * top[1][0] + side[0][1] * top[1][1])
    cc = c - (side[1][0] * top[1][0] + side[1][1] * top[1][1])
    return [
        [aa, bb, side[0][0], side[0][1]],
        [bb, cc, side[1][0], side[1][1]],
        [side[0][0], side[1][0], p, q],
        [side[0][1], side[1][1], q, r],
    ]


def small_inverse(block, begin=0, end=None):
    size = block.shape[0]
    end = size if end is None else end
    down = lax.broadcasted_iota(jnp.int32, (size, size), 0)
    across = lax.broadcasted_iota(jnp.int32, (size, size), 1)
    lane = across[0:8]

    def spread(values, j):
        return [jnp.broadcast_to(values[:, j + k:j + k + 1], (size, size)) for k in range(4)]

    def tall(row):
        return jnp.concatenate([row] * (size // 8), axis=0)

    def mix(weights, rows):
        return (weights[0] * rows[0] + weights[1] * rows[1]) + (weights[2] * rows[2] + weights[3] * rows[3])

    cols = spread(block, begin)
    for j in range(begin, end, 4):
        later = spread(block, j + 4) if j + 4 < end else []
        pivot = [[jnp.broadcast_to(cols[max(k, l)][j + min(k, l):j + min(k, l) + 1], (8, size)) for l in range(4)] for k in range(4)]
        inverse = inverse_4x4(pivot)
        ahead = []
        for old in later:
            here = [jnp.broadcast_to(old[j + k:j + k + 1], (8, size)) for k in range(4)]
            new_rows = [tall(mix(inverse[k], here)) for k in range(4)]
            new = old - mix(cols, new_rows)
            for k in range(4):
                new = jnp.where(down == j + k, new_rows[k], new)
            ahead.append(new)
        rows = [jnp.broadcast_to(block[j + k:j + k + 1], (8, size)) for k in range(4)]
        done = []
        for k in range(4):
            row = mix(inverse[k], rows)
            for l in range(4):
                row = jnp.where(lane == j + l, inverse[k][l], row)
            done.append(tall(row))
        block = jnp.where((across >= j) & (across < j + 4), 0.0, block) - mix(cols, done)
        for k in range(4):
            block = jnp.where(down == j + k, done[k], block)
        cols = ahead
    return block


def exact_dot(x, y):
    return jnp.dot(x, y, precision=lax.Precision.HIGHEST, preferred_element_type=jnp.float32)


def eliminate(inv, low, high, pivot=None):
    if pivot is None:
        pivot = small_inverse(inv[low:high, low:high])
    inv[low:high, :] = exact_dot(pivot, inv[low:high, :])
    inv[low:high, low:high] = pivot
    rows = inv[low:high, :]
    for part in ((0, low), (high, inv.shape[0])):
        if part[0] < part[1]:
            cols = inv[part[0]:part[1], low:high]
            inv[part[0]:part[1], low:high] = jnp.zeros_like(cols)
            inv[part[0]:part[1], :] = inv[part[0]:part[1], :] - exact_dot(cols, rows)


def kernel(
    obs_hbm, firsts, rows_s, cols_s, fac_hbm, out_ref, more_ref, fall0, fall1, obs_v, sel0, sel1, turn0, turn1, keeps, masked, eye,
    gram0, gram0_near, gram0_ring, gram1, gram1_near, gram1_ring, rhs0, rhs0_near, rhs0_ring, rhs1, rhs1_near, rhs1_ring,
    rhs_all, inv, whole_gram, corner, small, send_sem, recv_sem, loc_sem, sum_send, sum_recv
):
    wide = lax.axis_index("wide")
    narrow = lax.axis_index("narrow")
    my_y, my_z = wide // NZ, wide % NZ
    my_x, my_core = narrow // 2, narrow % 2
    own, order = order_of_arrival()
    number = {what: at for at, what in enumerate(order)}
    shard = fac_hbm.shape[0]
    slots = cols_s.shape[0]
    rank = fac_hbm.shape[2]
    half = rank // 2
    lanes, width = obs_v.shape[1:]
    part = lanes // 2
    groups = part // GROUP
    falls, sels, turns = (fall0, fall1), (sel0, sel1), (turn0, turn1)

    def device(dy, dz):
        return (((my_y + dy + NY) % NY) * NZ + (my_z + dz + NZ) % NZ, narrow)

    def beside(dx, other):
        core = 1 - my_core if other else my_core
        return (wide, (my_x + dx + NX) % NX * 2 + core)

    fac_copies = [
        pltpu.make_async_copy(
            fac_hbm.at[:, :, h * half:(h + 1) * half], falls[h].at[pl.ds(wide * shard, shard)], loc_sem.at[h]
        )
        for h in range(2)
    ]
    for one in fac_copies:
        one.start()
    obs_copy = pltpu.make_async_copy(obs_hbm, obs_v, loc_sem.at[2])
    obs_copy.start()

    barrier = pltpu.get_barrier_semaphore()
    partners = [device(*step) for step in ((1, 0), (-1, 0), (0, 1), (0, -1))]
    partners += [beside(0, 1), beside(1, 0), beside(-1, 0)]
    for partner in partners:
        pl.semaphore_signal(barrier, inc=1, device_id=partner, device_id_type=MESH)
    for one in fac_copies:
        one.wait()
    pl.semaphore_wait(barrier, len(partners))

    def copy(h, piece, node, to, step):
        at = number[(h, piece, to)]
        source = ((my_y - node[0] + NY) % NY) * NZ + (my_z - node[1] + NZ) % NZ
        place = falls[h].at[pl.ds(source * shard + PIECES[piece][5], PIECES[piece][6])]
        return pltpu.make_async_remote_copy(
            src_ref=place,
            dst_ref=place,
            send_sem=send_sem.at[at],
            recv_sem=recv_sem.at[at],
            device_id=device(*step),
            device_id_type=MESH,
        )

    sent = []

    def pass_on(h, piece, node, kid):
        sent.append(copy(h, piece, node, kid, (kid[0] - node[0], kid[1] - node[1])))
        sent[-1].start()

    for piece, kid in own:
        pass_on(0, piece, (0, 0), kid)

    down = lax.broadcasted_iota(jnp.int32, (rank, rank), 0)
    across = lax.broadcasted_iota(jnp.int32, (rank, rank), 1)
    lane = lax.broadcasted_iota(jnp.int32, (GROUP, lanes), 1)
    eye[...] = jnp.where(down == across, 1.0, 0.0)[:half, :half].astype(jnp.bfloat16)
    obs_copy.wait()

    gram_sums = [
        RowSum(gram0, gram0_near, gram0_ring, sum_send, sum_recv, 0, my_x, my_core, beside),
        RowSum(gram1, gram1_near, gram1_ring, sum_send, sum_recv, 10, my_x, my_core, beside),
    ]
    rhs_sums = [
        RowSum(rhs0, rhs0_near, rhs0_ring, sum_send, sum_recv, 20, my_x, my_core, beside),
        RowSum(rhs1, rhs1_near, rhs1_ring, sum_send, sum_recv, 30, my_x, my_core, beside),
    ]

    def select(h, step):
        for t in range(AT_ONCE):
            pair = step * AT_ONCE + t
            tile = jnp.concatenate(
                [falls[h][cols_s[pair * 2 + k] * groups + g] for k in range(2) for g in range(groups)], axis=0
            )
            sels[h][pair] = tile
            flat = lax.dot_general(eye[...], tile, (((1,), (1,)), ((), ())), preferred_element_type=jnp.float32)
            turns[h][pair] = flat.astype(jnp.bfloat16)

    pairs = WINDOW // 2

    def keep_of(row):
        first = firsts[row]
        for t in range(pairs):
            keep = [jnp.where(rows_s[(first + t) * 2 + k] == row, 1.0, 0.0) for k in range(2)]
            keeps[row, t] = jnp.where(lane < part, keep[0], keep[1]).astype(jnp.bfloat16)

    def mask(h, row):
        first = firsts[row]
        for t in range(pairs):
            keep = jnp.concatenate([keeps[row, t]] * (half // GROUP), axis=0)
            masked[row, :, t * lanes:(t + 1) * lanes] = turns[h][first + t] * keep

    def product(row, load):
        first, total = firsts[row], None
        for t in range(0, pairs, 2):
            both = [load(first + k) for k in range(t, min(t + 2, pairs))]
            left = masked[row, :, t * lanes:(t + len(both)) * lanes]
            right = both[0] if len(both) == 1 else jnp.concatenate(both, axis=0)
            one = jnp.dot(left, right, preferred_element_type=jnp.float32)
            total = one if total is None else total + one
        return total

    def gram_of(h, row):
        if h == 0:
            gram0[row] = product(row, lambda at: sel0[at])
        else:
            gram1[row] = product(row, lambda at: jnp.concatenate([sel0[at], sel1[at]], axis=1))

    def rhs_of(h, row, tile):
        at = slice(tile * rank, (tile + 1) * rank)
        (rhs0, rhs1)[h][row, :, at] = product(row, lambda pair: obs_v[pair, :, at])

    def row_of(q, other):
        return gram_sums[0].row((2 - q + NX) % NX, other)

    def near(sums, q):
        sums.near((2 - q + NX) % NX, q).start()

    wide_tiles = width // rank
    steps = slots // 2 // AT_ONCE
    jobs = []
    for step in range(steps):
        jobs.append(lambda step=step: select(0, step))
    def gram_job(q, other):
        mask(0, row_of(q, other))
        gram_of(0, row_of(q, other))
        if other:
            near(gram_sums[0], q)

    def rhs_job(q, other, tile):
        rhs_of(0, row_of(q, other), tile)
        if other and tile == wide_tiles - 1:
            near(rhs_sums[0], q)

    def start_upper():
        upper = jnp.concatenate(gram_sums[0].total(), axis=0)
        corner[...] = upper + jnp.where(down == across, LAMBDA_REG, 0.0)[:half, :half]
        inv[:half, :half] = corner[...]

    def stage(p, begin):
        at = slice(p * PANEL, (p + 1) * PANEL)
        if begin == 0:
            small[...] = corner[at, at]
        small[...] = small_inverse(small[...], begin, begin + 16)
        if begin + 16 == PANEL:
            eliminate(corner, p * PANEL, (p + 1) * PANEL, small[...])

    def rhs_jobs(other, few):
        return [functools.partial(rhs_job, q, other, tile) for q in few for tile in range(wide_tiles)]

    jobs += [functools.partial(gram_job, q, other) for other in (True, False) for q in range(NX)]
    jobs += rhs_jobs(True, range(NX))
    jobs += [functools.partial(gram_sums[0].fold, q) for q in range(NX)]
    jobs += rhs_jobs(False, range(2))
    jobs += [gram_sums[0].forward]
    jobs += rhs_jobs(False, range(2, NX))
    jobs += [start_upper]
    jobs += [functools.partial(stage, 0, begin) for begin in range(0, PANEL, 16)]
    jobs += [functools.partial(rhs_sums[0].fold, q) for q in range(NX)]
    jobs += [functools.partial(stage, 1, begin) for begin in range(0, PANEL, 16)]
    jobs += [rhs_sums[0].forward]

    pl.loop(0, RW)(keep_of)
    ready = max(at for at, what in enumerate(order) if what is not None and what[0] == 0)
    done = 0
    for at, what in enumerate(order):
        if what is None:
            for piece, kid in own:
                pass_on(1, piece, (0, 0), kid)
            continue
        h, piece, node = what
        copy(h, piece, node, node, (1, 0)).wait_recv()
        for kid in by_depth(piece, node):
            pass_on(h, piece, node, kid)
        while done < len(jobs) and at >= ready and done * (len(order) - 1 - ready) <= (at - ready) * len(jobs):
            jobs[done]()
            done += 1
    while done < len(jobs):
        jobs[done]()
        done += 1

    pl.loop(0, steps)(functools.partial(select, 1))

    @pl.loop(0, NX)
    def other_grams(q):
        mask(1, row_of(q, True))
        gram_of(1, row_of(q, True))
        near(gram_sums[1], q)

    @pl.loop(0, NX)
    def own_grams(q):
        mask(1, row_of(q, False))
        gram_of(1, row_of(q, False))

    def rhs_pair(q):
        for other in (True, False):
            for tile in range(wide_tiles):
                rhs_of(1, row_of(q, other), tile)
            if other:
                near(rhs_sums[1], q)

    for q in range(NX):
        gram_sums[1].fold(q)
    pl.loop(0, 2)(rhs_pair)
    gram_sums[1].forward()
    rhs_sums[1].fold(0)
    rhs_sums[1].fold(1)
    pl.loop(2, NX)(rhs_pair)
    rhs_sums[1].fold(2)
    rhs_sums[1].fold(3)

    rhs_all[:, :half] = jnp.concatenate(rhs_sums[0].total(), axis=0).T
    same = jnp.where(down == across, LAMBDA_REG, 0.0)
    lower = jnp.concatenate(gram_sums[1].total(), axis=0)
    inv[half:, :] = lower + same[half:, :]
    inv[:half, half:] = lower[:, :half].T
    whole_gram[...] = inv[...]
    eliminate(inv, 0, half, corner[...])
    rhs_sums[1].forward()
    for p in range(half // PANEL, rank // PANEL):
        eliminate(inv, p * PANEL, (p + 1) * PANEL)

    rhs_all[:, half:] = jnp.concatenate(rhs_sums[1].total(), axis=0).T
    for tile in range(wide_tiles):
        at = slice(tile * rank, (tile + 1) * rank)
        total = rhs_all[at]
        first = exact_dot(total, inv[...])
        out_ref[at] = first
        more_ref[at] = exact_dot(total - exact_dot(first, whole_gram[...]), inv[...])

    for sums in gram_sums + rhs_sums:
        sums.finish()
    for out in sent:
        out.wait_send()


def solved_row(obs, rows, cols, factors):
    slots, part, width = obs.shape
    rank = factors.shape[-1]
    half = rank // 2
    edges = len(order_of_arrival()[1])
    every = NY * NZ * RW * part // GROUP

    def sums(rows, cols):
        return [
            pltpu.VMEM((RW, rows, cols), jnp.float32),
            pltpu.VMEM((NX, rows, cols), jnp.float32),
            pltpu.VMEM((6, rows // 2, cols), jnp.float32),
        ]

    return pl.pallas_call(
        kernel,
        out_shape=(jax.ShapeDtypeStruct((width, rank), jnp.float32),) * 2,
        in_specs=[
            pl.BlockSpec(memory_space=pl.ANY),
            pl.BlockSpec(memory_space=pltpu.SMEM),
            pl.BlockSpec(memory_space=pltpu.SMEM),
            pl.BlockSpec(memory_space=pltpu.SMEM),
            pl.BlockSpec(memory_space=pl.ANY),
        ],
        out_specs=(pl.BlockSpec(memory_space=pltpu.VMEM),) * 2,
        scratch_shapes=[
            pltpu.VMEM((every, GROUP, half), jnp.bfloat16),
            pltpu.VMEM((every, GROUP, half), jnp.bfloat16),
            pltpu.VMEM((slots // 2, 2 * part, width), jnp.bfloat16),
            pltpu.VMEM((slots // 2, 2 * part, half), jnp.bfloat16),
            pltpu.VMEM((slots // 2, 2 * part, half), jnp.bfloat16),
            pltpu.VMEM((slots // 2, half, 2 * part), jnp.bfloat16),
            pltpu.VMEM((slots // 2, half, 2 * part), jnp.bfloat16),
            pltpu.VMEM((RW, WINDOW // 2, GROUP, 2 * part), jnp.bfloat16),
            pltpu.VMEM((RW, half, WINDOW * part), jnp.bfloat16),
            pltpu.VMEM((half, half), jnp.bfloat16),
            *sums(half, half),
            *sums(half, rank),
            *sums(half, width),
            *sums(half, width),
            pltpu.VMEM((width, rank), jnp.float32),
            pltpu.VMEM((rank, rank), jnp.float32),
            pltpu.VMEM((rank, rank), jnp.float32),
            pltpu.VMEM((half, half), jnp.float32),
            pltpu.VMEM((PANEL, PANEL), jnp.float32),
            pltpu.SemaphoreType.DMA((edges,)),
            pltpu.SemaphoreType.DMA((edges,)),
            pltpu.SemaphoreType.DMA((3,)),
            pltpu.SemaphoreType.DMA((40,)),
            pltpu.SemaphoreType.DMA((40,)),
        ],
        compiler_params=pltpu.CompilerParams(collective_id=0, has_side_effects=True, vmem_limit_bytes=60 * 1024 * 1024),
        name="solve_rows",
    )(
        obs.reshape(slots // 2, 2 * part, width),
        window_starts(rows),
        rows,
        cols,
        factors.reshape(-1, GROUP, rank),
    )


def window_starts(rows):
    before = jnp.sum((rows[None, :] < jnp.arange(RW, dtype=jnp.int32)[:, None]).astype(jnp.int32), axis=1)
    return jnp.minimum(before // 2, (rows.shape[0] - WINDOW) // 2)


def body(obs_blocks, obs_row, obs_col, factors):
    product, correction = solved_row(obs_blocks[0], obs_row[0], obs_col[0], factors)
    return (product + correction)[None]


def solution(mesh):
    placed = (
        P("wide", None, "narrow", None),
        P("wide", None),
        P("wide", None),
        P("wide", "narrow", None),
    )
    return jax.shard_map(
        body,
        mesh=mesh,
        in_specs=placed,
        out_specs=P(("wide", "narrow"), None, None),
        check_vma=False,
    )
```
